32 devices in a mesh: groups: 2 (over y), seq: 4 (over z), head: 2 (over x), rep: 2 (over core).
Axes of the slice: x: 2, y: 2, z: 4, core: 2. Of those that a mesh axis runs over, the one named last changes fastest.
Arguments:
- queries: bfloat16 [16384, 2, 128], P(('groups', 'seq', 'rep'), 'head'), parts along dimension 0, may hold values from -160 to 160
- key_rows: bfloat16 [16384, 2, 128], P(('groups', 'seq', 'rep'), 'head'), parts along dimension 0, may hold values from -14 to 14
- value_rows: bfloat16 [16384, 2, 128], P(('groups', 'seq', 'rep'), 'head'), parts along dimension 0, may hold values from -6 to 6
- pattern: int32 [128, 6], P('groups'), parts along dimension 0, may hold values from -1 to 63, as said below
Outputs:
- attended: bfloat16 [16384, 2, 128], P(('groups', 'seq', 'rep'), 'head'), parts along dimension 0
The draws below stay inside these ranges and needn't reach their ends.
There are 2 independent parts, one for each index of `groups`. The reference program is written for one: setup_inputs(seed, part) draws one part's arguments, and reference() takes and returns one part's arrays. A program takes and returns all parts, laid end to end along the dimension named above; each array names one. Nothing has to cross between parts.
Inputs may be any that keep to these rules, and one draw needn't show every extreme that they name: `pattern`: row n lists, in this order, blocks n, n - 1 and n + 1 taken cyclically over the 64 blocks, then 3 entries: some key blocks followed by -1 for the rest; entry 3 + j, when it is not -1, is one of the blocks ((n // 8 + 2 + j) % 8) * 8 to that plus 8 - 1.
All inputs are finite; a program needn't handle non-finite values.
Results may differ from the reference program's by a relative error of at most 0.0049.
Values may be sent and summed in bfloat16 or wider, within the bound.
No kernel may reach another device: no remote copies, remote signals or barrier semaphores. Data moves between devices by JAX's collectives and lax.ppermute only.
A program may use at most 64 MiB of HBM per device.

```python
import math
import jax
import jax.numpy as jnp
from jax import lax

HD = 128
BLOCK = 128
QB_DEV = 8
FAR_MAX = 3
ITERS = 2
SHARDS = 8
NBLK = 64
TOKENS = 8192
HEADS = 2


def key_fields(key):
    base_key = jax.random.fold_in(key, 7)
    token_scale = jnp.exp(jax.random.uniform(jax.random.fold_in(base_key, 2), (TOKENS, HEADS, 1), jnp.float32, math.log(0.3), math.log(3.0)))
    base = jnp.clip(jax.random.normal(jax.random.fold_in(base_key, 1), (TOKENS, HEADS, HD), jnp.float32), -4.5, 4.5)
    return base * token_scale


def draw_key_rows(key, part):
    rows = key_fields(key)
    return rows.astype(jnp.bfloat16)


def draw_queries(key, part):
    result = jnp.clip(jax.random.normal(jax.random.fold_in(key, 9), (TOKENS, HEADS, HD), jnp.float32), -4.5, 4.5)
    return result.astype(jnp.bfloat16)


def draw_pattern(key, part):
    blocks = jnp.arange(NBLK, dtype=jnp.int32)
    holder = blocks // QB_DEV
    window = jnp.stack([blocks, (blocks - 1) % NBLK, (blocks + 1) % NBLK], axis=1)
    counts = jax.random.randint(jax.random.fold_in(key, 1), (NBLK,), 0, FAR_MAX + 1)
    within = jax.random.randint(jax.random.fold_in(key, 2), (NBLK, FAR_MAX), 0, QB_DEV)
    slots = jnp.arange(FAR_MAX, dtype=jnp.int32)
    source = (holder[:, None] + 2 + slots[None, :]) % SHARDS
    far_rows = source * QB_DEV + within
    far_rows = jnp.where(slots[None, :] < counts[:, None], far_rows, -1)
    return jnp.concatenate([window, far_rows], axis=1).astype(jnp.int32)


def block_levels(stream_key, dims, split, low, top_value):
    gain = 1.0
    for axis_at, blocks in split:
        draws = jax.random.uniform(jax.random.fold_in(jax.random.fold_in(stream_key, 6), axis_at), (blocks,), jnp.float32, low / len(split), top_value / len(split))
        gain = gain * jnp.repeat(jnp.exp(draws), dims[axis_at] // blocks).reshape((-1,) + (1,) * (len(dims) - 1 - axis_at))
    return gain


def centred(rng, extent, deviation, limit, pieces=(), held_as=jnp.bfloat16):
    entries = deviation * jax.random.normal(rng, extent, jnp.float32)
    if pieces:
        entries = entries * block_levels(rng, extent, pieces, -0.22, 0.18)
    return jnp.clip(entries, -limit, limit).astype(held_as)


def setup_inputs(seed: int = 0, part: int = 0) -> dict:
    keys = jax.random.split(jax.random.key(seed), 5)
    own_keys = jax.random.split(jax.random.fold_in(keys[4], part), 5)
    queries = draw_queries(jax.random.fold_in(jax.random.fold_in(keys[4], part), 71), part)
    key_rows = draw_key_rows(jax.random.fold_in(jax.random.fold_in(keys[4], part), 71), part)
    value_rows = centred(own_keys[2], (TOKENS, HEADS, HD), 1.0, 6.0, ((0, 8), (1, 2)))
    pattern = draw_pattern(jax.random.fold_in(jax.random.fold_in(keys[4], part), 71), part)
    return {"queries": queries, "key_rows": key_rows, "value_rows": value_rows, "pattern": pattern}


def head_layer(query_head, key_head, value_head, pattern):
    block_count = pattern.shape[0]
    present = pattern >= 0
    key_index = jnp.where(present, pattern, 0).astype(jnp.int32)
    query_blocks = query_head.reshape(block_count, BLOCK, HD).astype(jnp.float32)
    key_blocks = key_head.reshape(block_count, BLOCK, HD)[key_index].astype(jnp.float32)
    scores = jnp.einsum('nqd,nlud->nqlu', query_blocks, key_blocks) / math.sqrt(HD)
    scores = jnp.where(present[:, None, :, None], scores, -jnp.inf)
    row_peak = lax.optimization_barrier(jnp.max(scores, axis=(2, 3), keepdims=True))
    weights = jnp.exp(scores - row_peak)
    weights = weights / lax.optimization_barrier(jnp.sum(weights, axis=(2, 3), keepdims=True))
    for number in range(ITERS):
        col_parts = lax.optimization_barrier(jnp.sum(weights, axis=1))
        col_sums = jnp.zeros((block_count, BLOCK), jnp.float32).at[key_index].add(col_parts)
        weights = weights / col_sums[key_index][:, None, :, :]
        weights = weights / lax.optimization_barrier(jnp.sum(weights, axis=(2, 3), keepdims=True))
    rounded = lax.optimization_barrier(weights.astype(jnp.bfloat16)).astype(jnp.float32)
    value_blocks = value_head.reshape(block_count, BLOCK, HD)[key_index].astype(jnp.float32)
    attended = jnp.einsum('nqlu,nlud->nqd', rounded, value_blocks)
    return attended.reshape(block_count * BLOCK, HD).astype(jnp.bfloat16)

def reference(queries, key_rows, value_rows, pattern):
    stacked = (jnp.moveaxis(queries, 1, 0), jnp.moveaxis(key_rows, 1, 0), jnp.moveaxis(value_rows, 1, 0))
    result = lax.map(lambda triple: head_layer(triple[0], triple[1], triple[2], pattern), stacked)
    return jnp.moveaxis(result, 0, 1)
```

```python
import math

import jax
import jax.numpy as jnp
from jax import lax
from jax.experimental import pallas as pl
from jax.experimental.pallas import tpu as pltpu
from jax.sharding import PartitionSpec as P

BLOCK = 128
ITERS = 2
VMEM = pl.BlockSpec(memory_space=pltpu.VMEM)
SMEM = pl.BlockSpec(memory_space=pltpu.SMEM)
LIMIT = 32 * 1024 * 1024


def block_rows(ref, index):
    start = index * BLOCK
    if not isinstance(index, int):
        start = pl.multiple_of(start, BLOCK)
    return ref[pl.ds(start, BLOCK), :]


def slot_blocks(i, blocks, within_ref, own, low, high, fars):
    before = low[...] if i == 0 else block_rows(own, i - 1)
    after = high[...] if i == blocks - 1 else block_rows(own, i + 1)
    listed = [block_rows(own, i), before, after]
    for slot, far in enumerate(fars):
        listed.append(block_rows(far, within_ref[i, slot]))
    return listed


def add_columns(sums_ref, index_ref, i, weights):
    for slot, weight in enumerate(weights):
        at = pl.ds(index_ref[i, slot], 1)
        sums_ref[at, :] += jnp.sum(weight, axis=0, keepdims=True)


def row_total(parts):
    total = parts[0]
    for part in parts[1:]:
        total = total + part
    return jnp.sum(total, axis=1, keepdims=True)


def score_kernel(blocks, index_ref, within_ref, bias_ref, q_ref, own, low, high, *rest):
    fars, (exp_ref, sums_ref) = rest[:-2], rest[-2:]
    sums_ref[...] = jnp.zeros_like(sums_ref)
    for i in range(blocks):
        query = block_rows(q_ref, i)
        scores = []
        for slot, key in enumerate(slot_blocks(i, blocks, within_ref, own, low, high, fars)):
            score = lax.dot_general(
                query, key, (((1,), (1,)), ((), ())), preferred_element_type=jnp.float32
            )
            scores.append(score * (1.0 / math.sqrt(key.shape[1])) + bias_ref[i, slot])
        peak = scores[0]
        for score in scores[1:]:
            peak = jnp.maximum(peak, score)
        peak = jnp.max(peak, axis=1, keepdims=True)
        exps = [jnp.exp(score - peak) for score in scores]
        for slot, value in enumerate(exps):
            exp_ref[i, slot] = value
        scale = 1.0 / row_total(exps)
        add_columns(sums_ref, index_ref, i, [value * scale for value in exps])


def scaled(exp_ref, index_ref, i, factor_refs):
    parts = []
    for slot in range(exp_ref.shape[1]):
        value = exp_ref[i, slot]
        for factor in factor_refs:
            value = value * factor[pl.ds(index_ref[i, slot], 1), :]
        parts.append(value)
    return parts


def round_kernel(blocks, index_ref, exp_ref, sum_a, sum_b, factor_ref, sums_ref):
    factor_ref[...] = 1.0 / (sum_a[...] + sum_b[...])
    sums_ref[...] = jnp.zeros_like(sums_ref)
    for i in range(blocks):
        parts = scaled(exp_ref, index_ref, i, [factor_ref])
        scale = 1.0 / row_total(parts)
        add_columns(sums_ref, index_ref, i, [part * scale for part in parts])


def output_kernel(
    blocks, index_ref, within_ref, exp_ref, factor_ref, sum_a, sum_b, own, low, high, *rest
):
    fars, (out_ref, last_ref) = rest[:-2], rest[-2:]
    last_ref[...] = 1.0 / (sum_a[...] + sum_b[...])
    for i in range(blocks):
        parts = scaled(exp_ref, index_ref, i, [factor_ref, last_ref])
        scale = 1.0 / row_total(parts)
        total = None
        for part, value in zip(
            parts, slot_blocks(i, blocks, within_ref, own, low, high, fars)
        ):
            term = jnp.dot(
                (part * scale).astype(jnp.bfloat16), value, preferred_element_type=jnp.float32
            )
            total = term if total is None else total + term
        out_ref[pl.ds(i * BLOCK, BLOCK), :] = total.astype(out_ref.dtype)


def shifted(x, axis, by):
    devices = lax.axis_size(axis)
    return lax.ppermute(x, axis, [(i, (i + by) % devices) for i in range(devices)])


def swapped(x):
    return lax.ppermute(x, "rep", [(0, 1), (1, 0)])


def over_seq(x):
    devices = lax.axis_size("seq")
    if devices <= 4:
        parts = [
            lax.ppermute(x, "seq", [(i, i ^ by) for i in range(devices)])
            for by in reversed(range(1, devices))
        ]
        for part in parts:
            x = x + part
        return x
    by = 1
    while by < devices:
        x = x + lax.ppermute(x, "seq", [(i, i ^ by) for i in range(devices)])
        by *= 2
    return x


def far_rows(x, rep):
    near = shifted(x, "seq", -1)
    beyond = shifted(x, "seq", -2)
    other = swapped(jnp.where(rep == 0, beyond, near))
    return near, other, beyond


def body(queries, key_rows, value_rows, pattern):
    tok_local, heads_local, width = queries.shape
    assert heads_local == 1
    blocks = tok_local // BLOCK
    list_len = pattern.shape[1]
    far_count = list_len - 3
    total_blocks = pattern.shape[0]
    axes = ("seq", "rep")
    shards = lax.axis_size(axes)
    position = lax.axis_index(axes)
    rep = lax.axis_index("rep")
    q = queries.reshape(tok_local, width)
    k = key_rows.reshape(tok_local, width)
    v = value_rows.reshape(tok_local, width)

    my_lists = lax.dynamic_slice_in_dim(pattern, position * blocks, blocks, 0)
    present = my_lists >= 0
    index = jnp.where(present, my_lists, 0)
    source = (position + 2 + jnp.arange(far_count, dtype=jnp.int32)) % shards
    within = jnp.where(present[:, 3:], my_lists[:, 3:] - source[None, :] * blocks, 0)
    bias = jnp.where(present, 0.0, -jnp.inf).astype(jnp.float32)

    k_far = far_rows(k, rep)
    edges_low = jnp.concatenate([k[-BLOCK:], v[-BLOCK:]], axis=1)
    edges_high = jnp.concatenate([k[:BLOCK], v[:BLOCK]], axis=1)
    low = shifted(edges_low, axes, 1)
    high = shifted(edges_high, axes, -1)

    exps, sums = pl.pallas_call(
        lambda *refs: score_kernel(blocks, *refs),
        out_shape=(
            jax.ShapeDtypeStruct((blocks, list_len, BLOCK, BLOCK), jnp.float32),
            jax.ShapeDtypeStruct((total_blocks, BLOCK), jnp.float32),
        ),
        in_specs=[SMEM] * 3 + [VMEM] * (4 + far_count),
        out_specs=(VMEM, VMEM),
        compiler_params=pltpu.CompilerParams(vmem_limit_bytes=LIMIT),
    )(index, within, bias, q, k, low[:, :width], high[:, :width], *k_far)

    v_in, sums = lax.optimization_barrier((v, sums))
    mine = over_seq(sums)
    v_far = far_rows(v_in, rep)
    factor, sums = pl.pallas_call(
        lambda *refs: round_kernel(blocks, *refs),
        out_shape=(
            jax.ShapeDtypeStruct((total_blocks, BLOCK), jnp.float32),
            jax.ShapeDtypeStruct((total_blocks, BLOCK), jnp.float32),
        ),
        in_specs=[SMEM] + [VMEM] * 3,
        out_specs=(VMEM, VMEM),
        compiler_params=pltpu.CompilerParams(vmem_limit_bytes=LIMIT),
    )(index, exps, mine, swapped(mine))

    mine = over_seq(sums)
    out = pl.pallas_call(
        lambda *refs: output_kernel(blocks, *refs),
        out_shape=jax.ShapeDtypeStruct((tok_local, width), jnp.bfloat16),
        in_specs=[SMEM] * 2 + [VMEM] * (7 + far_count),
        out_specs=VMEM,
        scratch_shapes=[pltpu.VMEM((total_blocks, BLOCK), jnp.float32)],
        compiler_params=pltpu.CompilerParams(vmem_limit_bytes=LIMIT),
    )(index, within, exps, factor, mine, swapped(mine), v, low[:, width:], high[:, width:], *v_far)
    return out.reshape(tok_local, heads_local, width)


def solution(mesh):
    in_specs = (
        P(("groups", "seq", "rep"), "head", None),
        P(("groups", "seq", "rep"), "head", None),
        P(("groups", "seq", "rep"), "head", None),
        P("groups", None),
    )
    out_specs = P(("groups", "seq", "rep"), "head", None)
    return jax.shard_map(body, mesh=mesh, in_specs=in_specs, out_specs=out_specs, check_vma=False)
```

```python
import math

import jax
import jax.numpy as jnp
from jax import lax
from jax.experimental import pallas as pl
from jax.experimental.pallas import tpu as pltpu
from jax.sharding import PartitionSpec as P

BLOCK = 128
ITERS = 2
VMEM = pl.BlockSpec(memory_space=pltpu.VMEM)
SMEM = pl.BlockSpec(memory_space=pltpu.SMEM)
LIMIT = 32 * 1024 * 1024


def block_rows(ref, index):
    start = index * BLOCK
    if not isinstance(index, int):
        start = pl.multiple_of(start, BLOCK)
    return ref[pl.ds(start, BLOCK), :]


def near_blocks(i, blocks, own, low, high):
    before = low[...] if i == 0 else block_rows(own, i - 1)
    after = high[...] if i == blocks - 1 else block_rows(own, i + 1)
    return [block_rows(own, i), before, after]


def far_blocks(i, within_ref, fars):
    return [block_rows(far, within_ref[i, slot]) for slot, far in enumerate(fars)]


def score(query, key):
    product = lax.dot_general(
        query, key, (((1,), (1,)), ((), ())), preferred_element_type=jnp.float32
    )
    return product * (1.0 / math.sqrt(key.shape[1]))


def add_columns(sums_ref, index_ref, i, weights):
    for slot, weight in enumerate(weights):
        at = pl.ds(index_ref[i, slot], 1)
        sums_ref[at, :] += jnp.sum(weight, axis=0, keepdims=True)


def row_total(parts):
    total = parts[0]
    for part in parts[1:]:
        total = total + part
    return jnp.sum(total, axis=1, keepdims=True)


def near_kernel(blocks, q_ref, own, score_ref):
    for i in range(blocks):
        query = block_rows(q_ref, i)
        for slot, other in enumerate((i, i - 1, i + 1)):
            if 0 <= other < blocks:
                score_ref[i, slot] = score(query, block_rows(own, other))


def score_kernel(blocks, index_ref, within_ref, bias_ref, q_ref, near_ref, low, high, *rest):
    fars, (exp_ref, sums_ref) = rest[:-2], rest[-2:]
    near = near_ref.shape[1]
    sums_ref[...] = jnp.zeros_like(sums_ref)
    for i in range(blocks):
        query = block_rows(q_ref, i)
        scores = [near_ref[i, 0]]
        scores.append(score(query, low[...]) if i == 0 else near_ref[i, 1])
        scores.append(score(query, high[...]) if i == blocks - 1 else near_ref[i, 2])
        for slot, key in enumerate(far_blocks(i, within_ref, fars)):
            scores.append(score(query, key) + bias_ref[i, near + slot])
        peak = scores[0]
        for part in scores[1:]:
            peak = jnp.maximum(peak, part)
        peak = jnp.max(peak, axis=1, keepdims=True)
        exps = [jnp.exp(part - peak) for part in scores]
        for slot, value in enumerate(exps):
            exp_ref[i, slot] = value
        scale = 1.0 / row_total(exps)
        add_columns(sums_ref, index_ref, i, [value * scale for value in exps])


def scaled(exp_ref, index_ref, i, factor_refs):
    parts = []
    for slot in range(exp_ref.shape[1]):
        value = exp_ref[i, slot]
        for factor in factor_refs:
            value = value * factor[pl.ds(index_ref[i, slot], 1), :]
        parts.append(value)
    return parts


def round_kernel(blocks, index_ref, exp_ref, sum_a, sum_b, factor_ref, sums_ref):
    factor_ref[...] = 1.0 / (sum_a[...] + sum_b[...])
    sums_ref[...] = jnp.zeros_like(sums_ref)
    for i in range(blocks):
        parts = scaled(exp_ref, index_ref, i, [factor_ref])
        scale = 1.0 / row_total(parts)
        add_columns(sums_ref, index_ref, i, [part * scale for part in parts])


def output_kernel(
    blocks, index_ref, within_ref, exp_ref, factor_ref, sum_a, sum_b, own, low, high, *rest
):
    fars, (out_ref, last_ref) = rest[:-2], rest[-2:]
    last_ref[...] = 1.0 / (sum_a[...] + sum_b[...])
    for i in range(blocks):
        parts = scaled(exp_ref, index_ref, i, [factor_ref, last_ref])
        scale = 1.0 / row_total(parts)
        total = None
        values = near_blocks(i, blocks, own, low, high) + far_blocks(i, within_ref, fars)
        for part, value in zip(parts, values):
            term = jnp.dot(
                (part * scale).astype(jnp.bfloat16), value, preferred_element_type=jnp.float32
            )
            total = term if total is None else total + term
        out_ref[pl.ds(i * BLOCK, BLOCK), :] = total.astype(out_ref.dtype)


def shifted(x, axis, by):
    devices = lax.axis_size(axis)
    return lax.ppermute(x, axis, [(i, (i + by) % devices) for i in range(devices)])


def swapped(x):
    return lax.ppermute(x, "rep", [(0, 1), (1, 0)])


def over_seq(x):
    devices = lax.axis_size("seq")
    if devices <= 4:
        parts = [
            lax.ppermute(x, "seq", [(i, i ^ by) for i in range(devices)])
            for by in reversed(range(1, devices))
        ]
        for part in parts:
            x = x + part
        return x
    by = 1
    while by < devices:
        x = x + lax.ppermute(x, "seq", [(i, i ^ by) for i in range(devices)])
        by *= 2
    return x


def far_rows(x):
    near = shifted(x, "seq", -1)
    beyond = shifted(x, "seq", -2)
    return near, beyond


def with_swap(near, beyond, rep):
    other = swapped(jnp.where(rep == 0, beyond, near))
    return near, other, beyond


def body(queries, key_rows, value_rows, pattern):
    tok_local, heads_local, width = queries.shape
    assert heads_local == 1
    blocks = tok_local // BLOCK
    list_len = pattern.shape[1]
    far_count = list_len - 3
    total_blocks = pattern.shape[0]
    axes = ("seq", "rep")
    shards = lax.axis_size(axes)
    position = lax.axis_index(axes)
    rep = lax.axis_index("rep")
    q = queries.reshape(tok_local, width)
    k = key_rows.reshape(tok_local, width)
    v = value_rows.reshape(tok_local, width)

    my_lists = lax.dynamic_slice_in_dim(pattern, position * blocks, blocks, 0)
    present = my_lists >= 0
    index = jnp.where(present, my_lists, 0)
    source = (position + 2 + jnp.arange(far_count, dtype=jnp.int32)) % shards
    within = jnp.where(present[:, 3:], my_lists[:, 3:] - source[None, :] * blocks, 0)
    bias = jnp.where(present, 0.0, -jnp.inf).astype(jnp.float32)

    edges_low = jnp.concatenate([k[-BLOCK:], v[-BLOCK:]], axis=1)
    edges_high = jnp.concatenate([k[:BLOCK], v[:BLOCK]], axis=1)
    beyond = shifted(k, "seq", -2)
    k_in, edges_low = lax.optimization_barrier((k, edges_low))
    k_pair = (shifted(k_in, "seq", -1), beyond)
    low = shifted(edges_low, axes, 1)
    high = shifted(edges_high, axes, -1)

    near_scores = pl.pallas_call(
        lambda *refs: near_kernel(blocks, *refs),
        out_shape=jax.ShapeDtypeStruct((blocks, 3, BLOCK, BLOCK), jnp.float32),
        in_specs=[VMEM] * 2,
        out_specs=VMEM,
        cost_estimate=pl.CostEstimate(flops=100663296, bytes_accessed=4194304, transcendentals=0),
        compiler_params=pltpu.CompilerParams(vmem_limit_bytes=LIMIT),
    )(q, k)

    near_scores, v_in, *k_pair = lax.optimization_barrier((near_scores, v, *k_pair))
    v_near = shifted(v_in, "seq", -1)
    k_far = with_swap(*k_pair, rep)
    exps, sums = pl.pallas_call(
        lambda *refs: score_kernel(blocks, *refs),
        out_shape=(
            jax.ShapeDtypeStruct((blocks, list_len, BLOCK, BLOCK), jnp.float32),
            jax.ShapeDtypeStruct((total_blocks, BLOCK), jnp.float32),
        ),
        in_specs=[SMEM] * 3 + [VMEM] * (4 + far_count),
        out_specs=(VMEM, VMEM),
        cost_estimate=pl.CostEstimate(flops=100663296, bytes_accessed=6291456, transcendentals=786432),
        compiler_params=pltpu.CompilerParams(vmem_limit_bytes=LIMIT),
    )(index, within, bias, q, near_scores, low[:, :width], high[:, :width], *k_far)

    v_in, sums = lax.optimization_barrier((v, sums))
    mine = over_seq(sums)
    v_beyond = shifted(v_in, "seq", -2)
    mine, v_near = lax.optimization_barrier((mine, v_near))
    v_far = with_swap(v_near, v_beyond, rep)
    factor, sums = pl.pallas_call(
        lambda *refs: round_kernel(blocks, *refs),
        out_shape=(
            jax.ShapeDtypeStruct((total_blocks, BLOCK), jnp.float32),
            jax.ShapeDtypeStruct((total_blocks, BLOCK), jnp.float32),
        ),
        in_specs=[SMEM] + [VMEM] * 3,
        out_specs=(VMEM, VMEM),
        cost_estimate=pl.CostEstimate(flops=7864320, bytes_accessed=4194304, transcendentals=0),
        compiler_params=pltpu.CompilerParams(vmem_limit_bytes=LIMIT),
    )(index, exps, mine, swapped(mine))

    mine = over_seq(sums)
    out = pl.pallas_call(
        lambda *refs: output_kernel(blocks, *refs),
        out_shape=jax.ShapeDtypeStruct((tok_local, width), jnp.bfloat16),
        in_specs=[SMEM] * 2 + [VMEM] * (7 + far_count),
        out_specs=VMEM,
        scratch_shapes=[pltpu.VMEM((total_blocks, BLOCK), jnp.float32)],
        cost_estimate=pl.CostEstimate(flops=201326592, bytes_accessed=6291456, transcendentals=0),
        compiler_params=pltpu.CompilerParams(vmem_limit_bytes=LIMIT),
    )(index, within, exps, factor, mine, swapped(mine), v, low[:, width:], high[:, width:], *v_far)
    return out.reshape(tok_local, heads_local, width)


def solution(mesh):
    in_specs = (
        P(("groups", "seq", "rep"), "head", None),
        P(("groups", "seq", "rep"), "head", None),
        P(("groups", "seq", "rep"), "head", None),
        P("groups", None),
    )
    out_specs = P(("groups", "seq", "rep"), "head", None)
    return jax.shard_map(body, mesh=mesh, in_specs=in_specs, out_specs=out_specs, check_vma=False)
```

```python
import math

import jax
import jax.numpy as jnp
from jax import lax
from jax.experimental import pallas as pl
from jax.experimental.pallas import tpu as pltpu
from jax.sharding import PartitionSpec as P

BLOCK = 128
ITERS = 2
VMEM = pl.BlockSpec(memory_space=pltpu.VMEM)
ANY = pl.BlockSpec(memory_space=pl.ANY)
HBM = pl.BlockSpec(memory_space=pltpu.HBM)
SMEM = pl.BlockSpec(memory_space=pltpu.SMEM)
LIMIT = 32 * 1024 * 1024


def block_rows(ref, index):
    start = index * BLOCK
    if not isinstance(index, int):
        start = pl.multiple_of(start, BLOCK)
    return ref[pl.ds(start, BLOCK), :]


def near_blocks(i, blocks, own, low, high):
    before = low[...] if i == 0 else block_rows(own, i - 1)
    after = high[...] if i == blocks - 1 else block_rows(own, i + 1)
    return [block_rows(own, i), before, after]


def far_blocks(i, within_ref, fars):
    return [block_rows(far, within_ref[i, slot]) for slot, far in enumerate(fars)]


def score(query, key):
    product = lax.dot_general(
        query, key, (((1,), (1,)), ((), ())), preferred_element_type=jnp.float32
    )
    return product * (1.0 / math.sqrt(key.shape[1]))


def add_columns(sums_ref, lists_ref, i, weights):
    for slot, weight in enumerate(weights):
        at = pl.ds(jnp.maximum(lists_ref[i, slot], 0), 1)
        sums_ref[at, :] += jnp.sum(weight, axis=0, keepdims=True)


def row_total(parts):
    total = parts[0]
    for part in parts[1:]:
        total = total + part
    return jnp.sum(total, axis=1, keepdims=True)


def listed_bits(pattern_ref, blocks, shards, source, first_core):
    wanted = jnp.int32(0)
    for back, column, counted in ((4, 5, True), (3, 4, first_core)):
        if counted is False:
            continue
        first = (source + shards - back) % shards * blocks
        for i in range(blocks):
            entry = pattern_ref[column, first + i]
            bit = jnp.left_shift(jnp.int32(1), jnp.maximum(entry - source * blocks, 0))
            hit = entry >= 0 if counted is True else (entry >= 0) & counted
            wanted = jnp.where(hit, wanted | bit, wanted)
    return [jnp.bitwise_and(jnp.right_shift(wanted, b), 1) for b in range(blocks)]


class Copies:
    def __init__(self, sems):
        self.sems, self.started = sems, []

    def start(self, source, target):
        copy = pltpu.make_async_copy(source, target, self.sems.at[len(self.started)])
        copy.start()
        self.started.append(copy)

    def wait(self):
        for copy in self.started:
            copy.wait()


def pack(pattern_ref, blocks, shards, caps, rows, outs, order_ref, copies):
    position, rep = lax.axis_index(("seq", "rep")), lax.axis_index("rep")
    bits = listed_bits(pattern_ref, blocks, shards, position, rep == 0)
    rank, spare = jnp.int32(0), sum(bits)
    for b, bit in enumerate(bits):
        order_ref[jnp.where(bit == 1, rank, spare)] = b
        rank, spare = rank + bit, spare + 1 - bit
    for out, first in zip(outs, (0, 0, caps[1])):
        for t in range(out.shape[0] // BLOCK):
            begin = pl.multiple_of(order_ref[first + t] * BLOCK, BLOCK)
            copies.start(rows.at[pl.ds(begin, BLOCK), :], out.at[pl.ds(t * BLOCK, BLOCK), :])


def load(source, target, sem):
    copy = pltpu.make_async_copy(source, target, sem)
    copy.start()
    copy.wait()


def key_kernel(blocks, shards, caps, pattern_hbm, k_ref, *refs):
    outs, (pattern_ref, order_ref, sems, sem) = refs[:3], refs[3:]
    load(pattern_hbm, pattern_ref, sem)
    copies = Copies(sems)
    pack(pattern_ref, blocks, shards, caps, k_ref, outs, order_ref, copies)
    copies.wait()


def plan_kernel(blocks, shards, caps, pattern_hbm, k_ref, v_ref, *refs):
    outs, edges = refs[:3], refs[3:5]
    lists_ref, within_ref, crowded_ref, pattern_ref, order_ref, rank_ref, sems, sem = refs[5:]
    position, rep = lax.axis_index(("seq", "rep")), lax.axis_index("rep")
    width = k_ref.shape[1]
    copies = Copies(sems)
    for edge, begin in zip(edges, ((blocks - 1) * BLOCK, 0)):
        for at, rows in enumerate((k_ref, v_ref)):
            copies.start(rows.at[pl.ds(begin, BLOCK), :], edge.at[:, pl.ds(at * width, width)])
    load(pattern_hbm, pattern_ref, sem)
    pack(pattern_ref, blocks, shards, caps, v_ref, outs, order_ref, copies)
    for at, ahead in enumerate((3, 4)):
        source = lax.rem(position + ahead, shards)
        bits = listed_bits(
            pattern_ref, blocks, shards, source, (rep == 0) if ahead == 4 else True
        )
        rank = jnp.int32(0)
        for b, bit in enumerate(bits):
            rank_ref[at, b] = rank if ahead == 4 else jnp.where(rep == 1, rank, b)
            rank = rank + bit
    for i in range(blocks):
        for slot in range(pattern_ref.shape[0]):
            entry = pattern_ref[slot, position * blocks + i]
            lists_ref[i, slot] = entry
            if slot >= 3:
                source = lax.rem(position + slot - 1, shards)
                at = jnp.where(entry >= 0, entry - source * blocks, 0)
                within_ref[i, slot - 3] = at if slot == 3 else rank_ref[slot - 4, at]
    crowded = jnp.int32(0)
    for source in range(shards):
        count = sum(listed_bits(pattern_ref, blocks, shards, source, source % 2 == 0))
        crowded = jnp.maximum(crowded, jnp.where(count > caps[source % 2], 1, 0))
    crowded_ref[0] = crowded
    copies.wait()


def packed_shapes(blocks, caps, rows):
    sizes = (caps[0], caps[1], blocks - caps[1])
    return [jax.ShapeDtypeStruct((n * BLOCK, rows.shape[1]), rows.dtype) for n in sizes]


def pack_keys(blocks, shards, caps, columns, k):
    return pl.pallas_call(
        lambda *refs: key_kernel(blocks, shards, caps, *refs),
        out_shape=packed_shapes(blocks, caps, k),
        in_specs=[HBM] * 2,
        out_specs=[VMEM] * 3,
        scratch_shapes=[
            pltpu.SMEM(columns.shape, jnp.int32),
            pltpu.SMEM((blocks,), jnp.int32),
            pltpu.SemaphoreType.DMA((2 * blocks,)),
            pltpu.SemaphoreType.DMA,
        ],
    )(columns, k)


def plan(blocks, shards, caps, columns, k, v):
    width, list_len = k.shape[1], columns.shape[0]
    return pl.pallas_call(
        lambda *refs: plan_kernel(blocks, shards, caps, *refs),
        out_shape=packed_shapes(blocks, caps, v)
        + [jax.ShapeDtypeStruct((BLOCK, 2 * width), k.dtype)] * 2
        + [
            jax.ShapeDtypeStruct((blocks, list_len), jnp.int32),
            jax.ShapeDtypeStruct((blocks, list_len - 3), jnp.int32),
            jax.ShapeDtypeStruct((1,), jnp.int32),
        ],
        in_specs=[HBM] * 3,
        out_specs=[VMEM] * 5 + [SMEM] * 3,
        scratch_shapes=[
            pltpu.SMEM(columns.shape, jnp.int32),
            pltpu.SMEM((blocks,), jnp.int32),
            pltpu.SMEM((2, blocks), jnp.int32),
            pltpu.SemaphoreType.DMA((2 * blocks + 4,)),
            pltpu.SemaphoreType.DMA,
        ],
    )(columns, k, v)


def gather(rep, caps, wide, slim, rest, whole, sems, act):
    for core, first, skip in ((0, wide, caps[0] - caps[1]), (1, slim, 0)):

        @pl.when(rep == core)
        def _():
            used = first.shape[0]
            left = whole.shape[0] - used
            act(pltpu.make_async_copy(first, whole.at[pl.ds(0, used), :], sems.at[0]))
            act(
                pltpu.make_async_copy(
                    rest.at[pl.ds(skip * BLOCK, left), :], whole.at[pl.ds(used, left), :], sems.at[1]
                )
            )


def present(scores, entry):
    return scores + jnp.where(entry >= 0, 0.0, -jnp.inf).astype(jnp.float32)


def near_kernel(blocks, q_hbm, k_hbm, score_ref, q_ref, own, sems):
    copies = Copies(sems)
    copies.start(q_hbm, q_ref)
    copies.start(k_hbm, own)
    copies.wait()
    for i in range(blocks):
        query = block_rows(q_ref, i)
        for slot, other in enumerate((i, i - 1, i + 1)):
            if 0 <= other < blocks:
                score_ref[i, slot] = score(query, block_rows(own, other))


def score_kernel(
    blocks, caps, lists_ref, within_ref, q_ref, near_ref, low, high,
    near_far, other_far, wide, slim, rest, exp_ref, sums_ref, whole, sems,
):
    rep = lax.axis_index("rep")
    gather(rep, caps, wide, slim, rest, whole, sems, lambda copy: copy.start())
    near = near_ref.shape[1]
    sums_ref[...] = jnp.zeros_like(sums_ref)
    for i in range(blocks):
        query = block_rows(q_ref, i)
        for slot, key in enumerate(far_blocks(i, within_ref, (near_far, other_far))):
            exp_ref[i, near + slot] = present(score(query, key), lists_ref[i, near + slot])
    gather(rep, caps, wide, slim, rest, whole, sems, lambda copy: copy.wait())
    for i in range(blocks):
        query = block_rows(q_ref, i)
        scores = [near_ref[i, 0]]
        scores.append(score(query, low[...]) if i == 0 else near_ref[i, 1])
        scores.append(score(query, high[...]) if i == blocks - 1 else near_ref[i, 2])
        scores.extend([exp_ref[i, near], exp_ref[i, near + 1]])
        last = score(query, block_rows(whole, within_ref[i, 2]))
        scores.append(present(last, lists_ref[i, near + 2]))
        peak = scores[0]
        for part in scores[1:]:
            peak = jnp.maximum(peak, part)
        peak = jnp.max(peak, axis=1, keepdims=True)
        exps = [jnp.exp(part - peak) for part in scores]
        for slot, value in enumerate(exps):
            exp_ref[i, slot] = value
        scale = 1.0 / row_total(exps)
        add_columns(sums_ref, lists_ref, i, [value * scale for value in exps])


def scaled(exp_ref, lists_ref, i, factor_refs):
    parts = []
    for slot in range(exp_ref.shape[1]):
        value = exp_ref[i, slot]
        for factor in factor_refs:
            value = value * factor[pl.ds(jnp.maximum(lists_ref[i, slot], 0), 1), :]
        parts.append(value)
    return parts


def round_kernel(blocks, lists_ref, exp_ref, sum_a, sum_b, factor_ref, sums_ref):
    factor_ref[...] = 1.0 / (sum_a[...] + sum_b[...])
    sums_ref[...] = jnp.zeros_like(sums_ref)
    for i in range(blocks):
        parts = scaled(exp_ref, lists_ref, i, [factor_ref])
        scale = 1.0 / row_total(parts)
        add_columns(sums_ref, lists_ref, i, [part * scale for part in parts])


def output_kernel(
    blocks, caps, lists_ref, within_ref, exp_ref, factor_ref, sum_a, sum_b, own, low, high,
    near_far, other_far, wide, slim, rest, out_ref, last_ref, whole, partial_ref, weight_ref, sems,
):
    rep = lax.axis_index("rep")
    gather(rep, caps, wide, slim, rest, whole, sems, lambda copy: copy.start())
    last_ref[...] = 1.0 / (sum_a[...] + sum_b[...])
    for i in range(blocks):
        parts = scaled(exp_ref, lists_ref, i, [factor_ref, last_ref])
        scale = 1.0 / row_total(parts)
        values = near_blocks(i, blocks, own, low, high)
        values += far_blocks(i, within_ref, (near_far, other_far))
        parts = [(part * scale).astype(jnp.bfloat16) for part in parts]
        total = None
        for part, value in zip(parts, values):
            term = jnp.dot(part, value, preferred_element_type=jnp.float32)
            total = term if total is None else total + term
        partial_ref[i] = total
        weight_ref[i] = parts[-1]
    gather(rep, caps, wide, slim, rest, whole, sems, lambda copy: copy.wait())
    for i in range(blocks):
        value = block_rows(whole, within_ref[i, 2])
        total = partial_ref[i] + jnp.dot(weight_ref[i], value, preferred_element_type=jnp.float32)
        out_ref[pl.ds(i * BLOCK, BLOCK), :] = total.astype(out_ref.dtype)


def shifted(x, axis, by):
    devices = lax.axis_size(axis)
    return lax.ppermute(x, axis, [(i, (i + by) % devices) for i in range(devices)])


def swapped(x):
    return lax.ppermute(x, "rep", [(0, 1), (1, 0)])


def over_seq(x):
    devices = lax.axis_size("seq")
    if devices <= 4:
        parts = [
            lax.ppermute(x, "seq", [(i, i ^ by) for i in range(devices)])
            for by in reversed(range(1, devices))
        ]
        for part in parts:
            x = x + part
        return x
    by = 1
    while by < devices:
        x = x + lax.ppermute(x, "seq", [(i, i ^ by) for i in range(devices)])
        by *= 2
    return x


def two_away(wide, slim):
    chips = lax.axis_size("seq")
    moves = [(i, (i - 2) % chips) for i in range(chips)]
    axes = ("seq", "rep")
    return (
        lax.ppermute(wide, axes, [(2 * i, 2 * j) for i, j in moves]),
        lax.ppermute(slim, axes, [(2 * i + 1, 2 * j + 1) for i, j in moves]),
    )


def remainder(crowded, *rest):
    return lax.cond(
        crowded,
        lambda *x: tuple(shifted(part, "seq", -2) for part in x),
        lambda *x: tuple(jnp.zeros_like(part) for part in x),
        *rest,
    )


def with_swap(near, wide, rest, caps, rep):
    beyond = jnp.concatenate([wide, rest[(caps[0] - caps[1]) * BLOCK :]], axis=0)
    return swapped(jnp.where(rep == 0, beyond, near))


def body(queries, key_rows, value_rows, pattern):
    tok_local, heads_local, width = queries.shape
    assert heads_local == 1
    blocks = tok_local // BLOCK
    list_len = pattern.shape[1]
    far_count = list_len - 3
    total_blocks = pattern.shape[0]
    axes = ("seq", "rep")
    shards = lax.axis_size(axes)
    rep = lax.axis_index("rep")
    q = queries.reshape(tok_local, width)
    k = key_rows.reshape(tok_local, width)
    v = value_rows.reshape(tok_local, width)

    caps = (blocks - blocks // 8, blocks - 3 * blocks // 8)
    columns = pattern.T
    k_near = shifted(k, "seq", -1)
    k_wide, k_slim, k_rest = pack_keys(blocks, shards, caps, columns, k)
    k_in, columns, k_wide, k_slim, k_rest = lax.optimization_barrier(
        (k, columns, k_wide, k_slim, k_rest)
    )
    *v_packs, edges_low, edges_high, lists, within, crowded = plan(
        blocks, shards, caps, columns, k_in, v
    )
    v_wide, v_slim, v_rest = v_packs
    k_wide, k_slim = two_away(k_wide, k_slim)
    k_rest, v_rest = remainder(crowded[0] > 0, k_rest, v_rest)
    low = shifted(edges_low, axes, 1)
    high = shifted(edges_high, axes, -1)

    near_scores, q_held = pl.pallas_call(
        lambda *refs: near_kernel(blocks, *refs),
        out_shape=(
            jax.ShapeDtypeStruct((blocks, 3, BLOCK, BLOCK), jnp.float32),
            jax.ShapeDtypeStruct((tok_local, width), jnp.bfloat16),
        ),
        in_specs=[HBM] * 2,
        out_specs=(VMEM, VMEM),
        scratch_shapes=[
            pltpu.VMEM((tok_local, width), jnp.bfloat16),
            pltpu.SemaphoreType.DMA((2,)),
        ],
        cost_estimate=pl.CostEstimate(flops=100663296, bytes_accessed=4194304, transcendentals=0),
        compiler_params=pltpu.CompilerParams(vmem_limit_bytes=LIMIT),
    )(q, k)

    near_scores, v_in, k_near, k_wide, k_slim = lax.optimization_barrier(
        (near_scores, v, k_near, k_wide, k_slim)
    )
    v_near = shifted(v_in, "seq", -1)
    k_other = with_swap(k_near, k_wide, k_rest, caps, rep)
    exps, sums = pl.pallas_call(
        lambda *refs: score_kernel(blocks, caps, *refs),
        out_shape=(
            jax.ShapeDtypeStruct((blocks, list_len, BLOCK, BLOCK), jnp.float32),
            jax.ShapeDtypeStruct((total_blocks, BLOCK), jnp.float32),
        ),
        in_specs=[SMEM] * 2 + [VMEM] * 6 + [ANY] * 3,
        out_specs=(VMEM, VMEM),
        scratch_shapes=[
            pltpu.VMEM((tok_local, width), jnp.bfloat16),
            pltpu.SemaphoreType.DMA((2,)),
        ],
        cost_estimate=pl.CostEstimate(flops=100663296, bytes_accessed=6291456, transcendentals=786432),
        compiler_params=pltpu.CompilerParams(vmem_limit_bytes=LIMIT),
    )(
        lists, within, q_held, near_scores, low[:, :width], high[:, :width],
        k_near, k_other, k_wide, k_slim, k_rest,
    )

    v_wide, v_slim, sums = lax.optimization_barrier((v_wide, v_slim, sums))
    mine = over_seq(sums)
    v_wide, v_slim = two_away(v_wide, v_slim)
    mine, v_near = lax.optimization_barrier((mine, v_near))
    v_wide, v_slim = lax.optimization_barrier((v_wide, v_slim))
    v_other = with_swap(v_near, v_wide, v_rest, caps, rep)
    factor, sums = pl.pallas_call(
        lambda *refs: round_kernel(blocks, *refs),
        out_shape=(
            jax.ShapeDtypeStruct((total_blocks, BLOCK), jnp.float32),
            jax.ShapeDtypeStruct((total_blocks, BLOCK), jnp.float32),
        ),
        in_specs=[SMEM] + [VMEM] * 3,
        out_specs=(VMEM, VMEM),
        cost_estimate=pl.CostEstimate(flops=7864320, bytes_accessed=4194304, transcendentals=0),
        compiler_params=pltpu.CompilerParams(vmem_limit_bytes=LIMIT),
    )(lists, exps, mine, swapped(mine))

    mine = over_seq(sums)
    out = pl.pallas_call(
        lambda *refs: output_kernel(blocks, caps, *refs),
        out_shape=jax.ShapeDtypeStruct((tok_local, width), jnp.bfloat16),
        in_specs=[SMEM] * 2 + [VMEM] * 9 + [ANY] * 3,
        out_specs=VMEM,
        scratch_shapes=[
            pltpu.VMEM((total_blocks, BLOCK), jnp.float32),
            pltpu.VMEM((tok_local, width), jnp.bfloat16),
            pltpu.VMEM((blocks, BLOCK, width), jnp.float32),
            pltpu.VMEM((blocks, BLOCK, BLOCK), jnp.bfloat16),
            pltpu.SemaphoreType.DMA((2,)),
        ],
        cost_estimate=pl.CostEstimate(flops=201326592, bytes_accessed=6291456, transcendentals=0),
        compiler_params=pltpu.CompilerParams(vmem_limit_bytes=LIMIT),
    )(
        lists, within, exps, factor, mine, swapped(mine), v, low[:, width:], high[:, width:],
        v_near, v_other, v_wide, v_slim, v_rest,
    )
    return out.reshape(tok_local, heads_local, width)


def solution(mesh):
    in_specs = (
        P(("groups", "seq", "rep"), "head", None),
        P(("groups", "seq", "rep"), "head", None),
        P(("groups", "seq", "rep"), "head", None),
        P("groups", None),
    )
    out_specs = P(("groups", "seq", "rep"), "head", None)
    return jax.shard_map(body, mesh=mesh, in_specs=in_specs, out_specs=out_specs, check_vma=False)
```

```python
import math

import jax
import jax.numpy as jnp
from jax import lax
from jax.experimental import pallas as pl
from jax.experimental.pallas import tpu as pltpu
from jax.sharding import PartitionSpec as P

BLOCK = 128
ITERS = 2
LISTED = 6
SENT = jnp.float32
VMEM = pl.BlockSpec(memory_space=pltpu.VMEM)
ANY = pl.BlockSpec(memory_space=pl.ANY)
HBM = pl.BlockSpec(memory_space=pltpu.HBM)
SMEM = pl.BlockSpec(memory_space=pltpu.SMEM)
LIMIT = 32 * 1024 * 1024


def block_rows(ref, index):
    start = index * BLOCK
    if not isinstance(index, int):
        start = pl.multiple_of(start, BLOCK)
    return ref[pl.ds(start, BLOCK), :]


def near_blocks(i, blocks, own, low, high):
    before = low[...] if i == 0 else block_rows(own, i - 1)
    after = high[...] if i == blocks - 1 else block_rows(own, i + 1)
    return [block_rows(own, i), before, after]


def far_blocks(i, lists_ref, fars):
    return [block_rows(far, lists_ref[i, LISTED + slot]) for slot, far in enumerate(fars)]


def score(query, key):
    product = lax.dot_general(
        query, key, (((1,), (1,)), ((), ())), preferred_element_type=jnp.float32
    )
    return product * (1.0 / math.sqrt(key.shape[1]))


def add_columns(sums_ref, lists_ref, i, weights):
    for slot, weight in enumerate(weights):
        at = pl.ds(jnp.maximum(lists_ref[i, slot], 0), 1)
        sums_ref[at, :] += jnp.sum(weight, axis=0, keepdims=True)


def row_total(parts):
    total = parts[0]
    for part in parts[1:]:
        total = total + part
    return jnp.sum(total, axis=1, keepdims=True)


def listed_bits(pattern_ref, blocks, shards, source, first_core):
    wanted = jnp.int32(0)
    for back, column, counted in ((4, 5, True), (3, 4, first_core)):
        if counted is False:
            continue
        first = (source + shards - back) % shards * blocks
        for i in range(blocks):
            entry = pattern_ref[column, first + i]
            bit = jnp.left_shift(jnp.int32(1), jnp.maximum(entry - source * blocks, 0))
            hit = entry >= 0 if counted is True else (entry >= 0) & counted
            wanted = jnp.where(hit, wanted | bit, wanted)
    return [jnp.bitwise_and(jnp.right_shift(wanted, b), 1) for b in range(blocks)]


class Copies:
    def __init__(self, sems):
        self.sems, self.started = sems, []

    def start(self, source, target):
        copy = pltpu.make_async_copy(source, target, self.sems.at[len(self.started)])
        copy.start()
        self.started.append(copy)

    def wait(self):
        for copy in self.started:
            copy.wait()


def pack(pattern_ref, blocks, shards, caps, rows, outs, order_ref, copies):
    position, rep = lax.axis_index(("seq", "rep")), lax.axis_index("rep")
    bits = listed_bits(pattern_ref, blocks, shards, position, rep == 0)
    rank, spare = jnp.int32(0), sum(bits)
    for b, bit in enumerate(bits):
        order_ref[jnp.where(bit == 1, rank, spare)] = b
        rank, spare = rank + bit, spare + 1 - bit
    for out, first in zip(outs, (0, 0, caps[1])):
        for t in range(out.shape[0] // BLOCK):
            begin = pl.multiple_of(order_ref[first + t] * BLOCK, BLOCK)
            copies.start(rows.at[pl.ds(begin, BLOCK), :], out.at[pl.ds(t * BLOCK, BLOCK), :])


def load(source, target, sem):
    copy = pltpu.make_async_copy(source, target, sem)
    copy.start()
    copy.wait()


def key_kernel(blocks, shards, caps, pattern_hbm, k_ref, *refs):
    outs, (pattern_ref, order_ref, sems, sem) = refs[:3], refs[3:]
    load(pattern_hbm, pattern_ref, sem)
    copies = Copies(sems)
    pack(pattern_ref, blocks, shards, caps, k_ref, outs, order_ref, copies)
    copies.wait()


def plan_kernel(blocks, shards, caps, pattern_hbm, q_hbm, k_ref, v_ref, *refs):
    outs, edges = refs[:3], refs[3:5]
    score_ref, q_ref, lists_ref, crowded_ref = refs[5:9]
    own, pattern_ref, order_ref, rank_ref, sems, near_sems, sem = refs[9:]
    position, rep = lax.axis_index(("seq", "rep")), lax.axis_index("rep")
    width = k_ref.shape[1]
    held = Copies(near_sems)
    held.start(q_hbm, q_ref)
    held.start(k_ref, own)
    copies = Copies(sems)
    for edge, begin in zip(edges, ((blocks - 1) * BLOCK, 0)):
        for at, rows in enumerate((k_ref, v_ref)):
            copies.start(rows.at[pl.ds(begin, BLOCK), :], edge.at[:, pl.ds(at * width, width)])
    load(pattern_hbm, pattern_ref, sem)
    pack(pattern_ref, blocks, shards, caps, v_ref, outs, order_ref, copies)
    for at, ahead in enumerate((3, 4)):
        source = lax.rem(position + ahead, shards)
        bits = listed_bits(
            pattern_ref, blocks, shards, source, (rep == 0) if ahead == 4 else True
        )
        rank = jnp.int32(0)
        for b, bit in enumerate(bits):
            rank_ref[at, b] = rank if ahead == 4 else jnp.where(rep == 1, rank, b)
            rank = rank + bit
    for i in range(blocks):
        for slot in range(pattern_ref.shape[0]):
            entry = pattern_ref[slot, position * blocks + i]
            lists_ref[i, slot] = entry
            if slot >= 3:
                source = lax.rem(position + slot - 1, shards)
                at = jnp.where(entry >= 0, entry - source * blocks, 0)
                at = at if slot == 3 else rank_ref[slot - 4, at]
                lists_ref[i, pattern_ref.shape[0] + slot - 3] = at
    crowded = jnp.int32(0)
    for source in range(shards):
        count = sum(listed_bits(pattern_ref, blocks, shards, source, source % 2 == 0))
        crowded = jnp.maximum(crowded, jnp.where(count > caps[source % 2], 1, 0))
    crowded_ref[0] = crowded
    held.wait()
    for i in range(blocks):
        query = block_rows(q_ref, i)
        for slot, other in enumerate((i, i - 1, i + 1)):
            if 0 <= other < blocks:
                score_ref[i, slot] = score(query, block_rows(own, other))
    copies.wait()


def packed_shapes(blocks, caps, rows):
    sizes = (caps[0], caps[1], blocks - caps[1])
    return [jax.ShapeDtypeStruct((n * BLOCK, rows.shape[1]), rows.dtype) for n in sizes]


def pack_keys(blocks, shards, caps, columns, k):
    return pl.pallas_call(
        lambda *refs: key_kernel(blocks, shards, caps, *refs),
        out_shape=packed_shapes(blocks, caps, k),
        in_specs=[HBM] * 2,
        out_specs=[VMEM] * 3,
        scratch_shapes=[
            pltpu.SMEM(columns.shape, jnp.int32),
            pltpu.SMEM((blocks,), jnp.int32),
            pltpu.SemaphoreType.DMA((2 * blocks,)),
            pltpu.SemaphoreType.DMA,
        ],
    )(columns, k)


def plan(blocks, shards, caps, columns, q, k, v):
    width, list_len = k.shape[1], columns.shape[0]
    return pl.pallas_call(
        lambda *refs: plan_kernel(blocks, shards, caps, *refs),
        out_shape=packed_shapes(blocks, caps, v)
        + [jax.ShapeDtypeStruct((BLOCK, 2 * width), k.dtype)] * 2
        + [
            jax.ShapeDtypeStruct((blocks, 3, BLOCK, BLOCK), jnp.float32),
            jax.ShapeDtypeStruct(q.shape, q.dtype),
            jax.ShapeDtypeStruct((blocks, 2 * list_len - 3), jnp.int32),
            jax.ShapeDtypeStruct((1,), jnp.int32),
        ],
        in_specs=[HBM] * 4,
        out_specs=[VMEM] * 7 + [SMEM] * 2,
        scratch_shapes=[
            pltpu.VMEM(k.shape, k.dtype),
            pltpu.SMEM(columns.shape, jnp.int32),
            pltpu.SMEM((blocks,), jnp.int32),
            pltpu.SMEM((2, blocks), jnp.int32),
            pltpu.SemaphoreType.DMA((2 * blocks + 4,)),
            pltpu.SemaphoreType.DMA((2,)),
            pltpu.SemaphoreType.DMA,
        ],
        cost_estimate=pl.CostEstimate(flops=100663296, bytes_accessed=4194304, transcendentals=0),
        compiler_params=pltpu.CompilerParams(vmem_limit_bytes=LIMIT),
    )(columns, q, k, v)


class Whole:
    def __init__(self, caps, wide, slim, rest, whole, lists_hbm, lists_ref, sems):
        self.parts = (0, wide, caps[0] - caps[1]), (1, slim, 0)
        self.rest, self.whole, self.sem = rest, whole, sems.at[0]
        self.lists = pltpu.make_async_copy(lists_hbm, lists_ref, sems.at[1])

    def left(self, used, skip):
        count = self.whole.shape[0] - used
        return pltpu.make_async_copy(
            self.rest.at[pl.ds(skip * BLOCK, count), :], self.whole.at[pl.ds(used, count), :], self.sem
        )

    def on_core(self, act):
        for core, first, skip in self.parts:

            @pl.when(lax.axis_index("rep") == core)
            def _():
                act(first, skip)

    def start(self):
        self.lists.start()

        def begin(first, skip):
            self.left(first.shape[0], skip).start()
            self.whole[: first.shape[0], :] = first[...]

        self.on_core(begin)

    def wait(self):
        self.on_core(lambda first, skip: self.left(first.shape[0], skip).wait())


def present(scores, entry):
    return scores + jnp.where(entry >= 0, 0.0, -jnp.inf).astype(jnp.float32)


def score_kernel(
    blocks, caps, lists_hbm, q_ref, near_ref, low, high,
    near_far, other_far, wide, slim, rest, exp_ref, sums_ref, sent_ref,
    whole, lists_ref, sems,
):
    gathered = Whole(caps, wide, slim, rest, whole, lists_hbm, lists_ref, sems)
    gathered.start()
    near = near_ref.shape[1]
    sums_ref[...] = jnp.zeros_like(sums_ref)
    gathered.lists.wait()
    for i in range(blocks):
        query = block_rows(q_ref, i)
        for slot, key in enumerate(far_blocks(i, lists_ref, (near_far, other_far))):
            exp_ref[i, near + slot] = present(score(query, key), lists_ref[i, near + slot])
    gathered.wait()
    for i in range(blocks):
        query = block_rows(q_ref, i)
        scores = [near_ref[i, 0]]
        scores.append(score(query, low[...]) if i == 0 else near_ref[i, 1])
        scores.append(score(query, high[...]) if i == blocks - 1 else near_ref[i, 2])
        scores.extend([exp_ref[i, near], exp_ref[i, near + 1]])
        last = score(query, block_rows(whole, lists_ref[i, LISTED + 2]))
        scores.append(present(last, lists_ref[i, near + 2]))
        peak = scores[0]
        for part in scores[1:]:
            peak = jnp.maximum(peak, part)
        peak = jnp.max(peak, axis=1, keepdims=True)
        exps = [jnp.exp(part - peak) for part in scores]
        for slot, value in enumerate(exps):
            exp_ref[i, slot] = value
        scale = 1.0 / row_total(exps)
        add_columns(sums_ref, lists_ref, i, [value * scale for value in exps])
    sent_ref[...] = sums_ref[...].astype(sent_ref.dtype)


def scaled(exp_ref, lists_ref, i, factor_refs):
    parts = []
    for slot in range(exp_ref.shape[1]):
        value = exp_ref[i, slot]
        for factor in factor_refs:
            value = value * factor[pl.ds(jnp.maximum(lists_ref[i, slot], 0), 1), :]
        parts.append(value)
    return parts


def round_kernel(
    blocks, lists_hbm, exp_ref, sum_a, sum_b, factor_ref, sums_ref, sent_ref, lists_ref, sem
):
    load(lists_hbm, lists_ref, sem)
    factor_ref[...] = 1.0 / (sum_a[...] + sum_b[...].astype(jnp.float32))
    sums_ref[...] = jnp.zeros_like(sums_ref)
    for i in range(blocks):
        parts = scaled(exp_ref, lists_ref, i, [factor_ref])
        scale = 1.0 / row_total(parts)
        add_columns(sums_ref, lists_ref, i, [part * scale for part in parts])
    sent_ref[...] = sums_ref[...].astype(sent_ref.dtype)


def output_kernel(
    blocks, caps, lists_hbm, exp_ref, factor_ref, sum_a, sum_b, own, low, high,
    near_far, other_far, wide, slim, rest, out_ref, last_ref, whole, partial_ref, weight_ref,
    lists_ref, sems,
):
    gathered = Whole(caps, wide, slim, rest, whole, lists_hbm, lists_ref, sems)
    gathered.start()
    last_ref[...] = 1.0 / (sum_a[...] + sum_b[...].astype(jnp.float32))
    gathered.lists.wait()
    for i in range(blocks):
        parts = scaled(exp_ref, lists_ref, i, [factor_ref, last_ref])
        scale = 1.0 / row_total(parts)
        values = near_blocks(i, blocks, own, low, high)
        values += far_blocks(i, lists_ref, (near_far, other_far))
        parts = [(part * scale).astype(jnp.bfloat16) for part in parts]
        total = None
        for part, value in zip(parts, values):
            term = jnp.dot(part, value, preferred_element_type=jnp.float32)
            total = term if total is None else total + term
        partial_ref[i] = total
        weight_ref[i] = parts[-1]
    gathered.wait()
    for i in range(blocks):
        value = block_rows(whole, lists_ref[i, LISTED + 2])
        total = partial_ref[i] + jnp.dot(weight_ref[i], value, preferred_element_type=jnp.float32)
        out_ref[pl.ds(i * BLOCK, BLOCK), :] = total.astype(out_ref.dtype)


def shifted(x, axis, by):
    devices = lax.axis_size(axis)
    return lax.ppermute(x, axis, [(i, (i + by) % devices) for i in range(devices)])


def swapped(x):
    return lax.ppermute(x, "rep", [(0, 1), (1, 0)])


def over_seq(mine, sent):
    devices = lax.axis_size("seq")
    pairs = lambda by: [(i, i ^ by) for i in range(devices)]
    if devices <= 4:
        parts = [lax.ppermute(sent, "seq", pairs(by)) for by in reversed(range(1, devices))]
        return sum([part.astype(mine.dtype) for part in parts], mine)
    by = 1
    while by < devices:
        mine = mine + lax.ppermute(mine, "seq", pairs(by))
        by *= 2
    return mine


def two_away(wide, slim):
    chips = lax.axis_size("seq")
    moves = [(i, (i - 2) % chips) for i in range(chips)]
    axes = ("seq", "rep")
    return (
        lax.ppermute(wide, axes, [(2 * i, 2 * j) for i, j in moves]),
        lax.ppermute(slim, axes, [(2 * i + 1, 2 * j + 1) for i, j in moves]),
    )


def remainder(crowded, *rest):
    return lax.cond(
        crowded,
        lambda *x: tuple(shifted(part, "seq", -2) for part in x),
        lambda *x: x,
        *rest,
    )


def with_swap(near, wide, rest, caps, rep):
    beyond = jnp.concatenate([wide, rest[(caps[0] - caps[1]) * BLOCK :]], axis=0)
    return swapped(jnp.where(rep == 0, beyond, near))


def body(queries, key_rows, value_rows, pattern):
    tok_local, heads_local, width = queries.shape
    assert heads_local == 1
    blocks = tok_local // BLOCK
    list_len = pattern.shape[1]
    far_count = list_len - 3
    total_blocks = pattern.shape[0]
    axes = ("seq", "rep")
    shards = lax.axis_size(axes)
    rep = lax.axis_index("rep")
    q = queries.reshape(tok_local, width)
    k = key_rows.reshape(tok_local, width)
    v = value_rows.reshape(tok_local, width)

    caps = (blocks - blocks // 8, blocks - 3 * blocks // 8)
    columns = pattern.T
    k_near = shifted(k, "seq", -1)
    k_wide, k_slim, k_rest = pack_keys(blocks, shards, caps, columns, k)
    k_in, columns, k_wide, k_slim, k_rest = lax.optimization_barrier(
        (k, columns, k_wide, k_slim, k_rest)
    )
    *v_packs, edges_low, edges_high, near_scores, q_held, lists, crowded = plan(
        blocks, shards, caps, columns, q, k_in, v
    )
    v_wide, v_slim, v_rest = v_packs
    k_wide, k_slim = two_away(k_wide, k_slim)
    k_rest, v_rest = remainder(crowded[0] > 0, k_rest, v_rest)
    low = shifted(edges_low, axes, 1)
    high = shifted(edges_high, axes, -1)

    near_scores, v_in, k_near, k_wide, k_slim = lax.optimization_barrier(
        (near_scores, v, k_near, k_wide, k_slim)
    )
    v_near = shifted(v_in, "seq", -1)
    k_other = with_swap(k_near, k_wide, k_rest, caps, rep)
    exps, sums, sent = pl.pallas_call(
        lambda *refs: score_kernel(blocks, caps, *refs),
        out_shape=(
            jax.ShapeDtypeStruct((blocks, list_len, BLOCK, BLOCK), jnp.float32),
            jax.ShapeDtypeStruct((total_blocks, BLOCK), jnp.float32),
            jax.ShapeDtypeStruct((total_blocks, BLOCK), SENT),
        ),
        in_specs=[HBM] + [VMEM] * 8 + [ANY],
        out_specs=(VMEM, VMEM, VMEM),
        scratch_shapes=[
            pltpu.VMEM((tok_local, width), jnp.bfloat16),
            pltpu.SMEM((blocks, 2 * list_len - 3), jnp.int32),
            pltpu.SemaphoreType.DMA((2,)),
        ],
        cost_estimate=pl.CostEstimate(flops=100663296, bytes_accessed=6291456, transcendentals=786432),
        compiler_params=pltpu.CompilerParams(vmem_limit_bytes=LIMIT),
    )(
        lists, q_held, near_scores, low[:, :width], high[:, :width],
        k_near, k_other, k_wide, k_slim, k_rest,
    )

    v_wide, v_slim, sent = lax.optimization_barrier((v_wide, v_slim, sent))
    mine = over_seq(sums, sent)
    v_wide, v_slim = two_away(v_wide, v_slim)
    mine, v_near = lax.optimization_barrier((mine, v_near))
    v_wide, v_slim = lax.optimization_barrier((v_wide, v_slim))
    v_other = with_swap(v_near, v_wide, v_rest, caps, rep)
    factor, sums, sent = pl.pallas_call(
        lambda *refs: round_kernel(blocks, *refs),
        out_shape=(
            jax.ShapeDtypeStruct((total_blocks, BLOCK), jnp.float32),
            jax.ShapeDtypeStruct((total_blocks, BLOCK), jnp.float32),
            jax.ShapeDtypeStruct((total_blocks, BLOCK), SENT),
        ),
        in_specs=[HBM] + [VMEM] * 3,
        out_specs=(VMEM, VMEM, VMEM),
        scratch_shapes=[
            pltpu.SMEM((blocks, 2 * list_len - 3), jnp.int32),
            pltpu.SemaphoreType.DMA,
        ],
        cost_estimate=pl.CostEstimate(flops=7864320, bytes_accessed=4194304, transcendentals=0),
        compiler_params=pltpu.CompilerParams(vmem_limit_bytes=LIMIT),
    )(lists, exps, mine, swapped(mine.astype(SENT)))

    mine = over_seq(sums, sent)
    out = pl.pallas_call(
        lambda *refs: output_kernel(blocks, caps, *refs),
        out_shape=jax.ShapeDtypeStruct((tok_local, width), jnp.bfloat16),
        in_specs=[HBM] + [VMEM] * 11 + [ANY],
        out_specs=VMEM,
        scratch_shapes=[
            pltpu.VMEM((total_blocks, BLOCK), jnp.float32),
            pltpu.VMEM((tok_local, width), jnp.bfloat16),
            pltpu.VMEM((blocks, BLOCK, width), jnp.float32),
            pltpu.VMEM((blocks, BLOCK, BLOCK), jnp.bfloat16),
            pltpu.SMEM((blocks, 2 * list_len - 3), jnp.int32),
            pltpu.SemaphoreType.DMA((2,)),
        ],
        cost_estimate=pl.CostEstimate(flops=201326592, bytes_accessed=6291456, transcendentals=0),
        compiler_params=pltpu.CompilerParams(vmem_limit_bytes=LIMIT),
    )(
        lists, exps, factor, mine, swapped(mine.astype(SENT)), v, low[:, width:], high[:, width:],
        v_near, v_other, v_wide, v_slim, v_rest,
    )
    return out.reshape(tok_local, heads_local, width)


def solution(mesh):
    in_specs = (
        P(("groups", "seq", "rep"), "head", None),
        P(("groups", "seq", "rep"), "head", None),
        P(("groups", "seq", "rep"), "head", None),
        P("groups", None),
    )
    out_specs = P(("groups", "seq", "rep"), "head", None)
    return jax.shard_map(body, mesh=mesh, in_specs=in_specs, out_specs=out_specs, check_vma=False)
```

```python
import math

import jax
import jax.numpy as jnp
from jax import lax
from jax.experimental import pallas as pl
from jax.experimental.pallas import tpu as pltpu
from jax.sharding import PartitionSpec as P

BLOCK = 128
ITERS = 2
LISTED = 6
SENT = jnp.float32
VMEM = pl.BlockSpec(memory_space=pltpu.VMEM)
ANY = pl.BlockSpec(memory_space=pl.ANY)
HBM = pl.BlockSpec(memory_space=pltpu.HBM)
SMEM = pl.BlockSpec(memory_space=pltpu.SMEM)
LIMIT = 32 * 1024 * 1024


def block_rows(ref, index):
    start = index * BLOCK
    if not isinstance(index, int):
        start = pl.multiple_of(start, BLOCK)
    return ref[pl.ds(start, BLOCK), :]


def near_blocks(i, blocks, own, low, high):
    before = low[...] if i == 0 else block_rows(own, i - 1)
    after = high[...] if i == blocks - 1 else block_rows(own, i + 1)
    return [block_rows(own, i), before, after]


def far_blocks(i, lists_ref, fars):
    return [block_rows(far, lists_ref[i, LISTED + slot]) for slot, far in enumerate(fars)]


def score(query, key):
    product = lax.dot_general(
        query, key, (((1,), (1,)), ((), ())), preferred_element_type=jnp.float32
    )
    return product * (1.0 / math.sqrt(key.shape[1]))


def add_columns(sums_ref, lists_ref, i, weights):
    for slot, weight in enumerate(weights):
        at = pl.ds(jnp.maximum(lists_ref[i, slot], 0), 1)
        sums_ref[at, :] += jnp.sum(weight, axis=0, keepdims=True)


def row_total(parts):
    total = parts[0]
    for part in parts[1:]:
        total = total + part
    return jnp.sum(total, axis=1, keepdims=True)


def listed_bits(pattern_ref, blocks, shards, source, first_core):
    wanted = jnp.int32(0)
    for back, column, counted in ((4, 5, True), (3, 4, first_core)):
        if counted is False:
            continue
        first = (source + shards - back) % shards * blocks
        for i in range(blocks):
            entry = pattern_ref[column, first + i]
            bit = jnp.left_shift(jnp.int32(1), jnp.maximum(entry - source * blocks, 0))
            hit = entry >= 0 if counted is True else (entry >= 0) & counted
            wanted = jnp.where(hit, wanted | bit, wanted)
    return [jnp.bitwise_and(jnp.right_shift(wanted, b), 1) for b in range(blocks)]


class Copies:
    def __init__(self, sems):
        self.sems, self.started = sems, []

    def start(self, source, target):
        copy = pltpu.make_async_copy(source, target, self.sems.at[len(self.started)])
        copy.start()
        self.started.append(copy)

    def wait(self):
        for copy in self.started:
            copy.wait()


def pack(pattern_ref, blocks, shards, caps, rows, outs, order_ref, copies):
    position, rep = lax.axis_index(("seq", "rep")), lax.axis_index("rep")
    bits = listed_bits(pattern_ref, blocks, shards, position, rep == 0)
    rank, spare = jnp.int32(0), sum(bits)
    for b, bit in enumerate(bits):
        order_ref[jnp.where(bit == 1, rank, spare)] = b
        rank, spare = rank + bit, spare + 1 - bit
    for out, first in zip(outs, (0, 0, caps[1])):
        for t in range(out.shape[0] // BLOCK):
            begin = pl.multiple_of(order_ref[first + t] * BLOCK, BLOCK)
            copies.start(rows.at[pl.ds(begin, BLOCK), :], out.at[pl.ds(t * BLOCK, BLOCK), :])


def load(source, target, sem):
    copy = pltpu.make_async_copy(source, target, sem)
    copy.start()
    copy.wait()


def key_kernel(blocks, shards, caps, pattern_hbm, k_ref, *refs):
    outs, (pattern_ref, order_ref, sems, sem) = refs[:3], refs[3:]
    load(pattern_hbm, pattern_ref, sem)
    copies = Copies(sems)
    pack(pattern_ref, blocks, shards, caps, k_ref, outs, order_ref, copies)
    copies.wait()


def plan_kernel(blocks, shards, caps, pattern_hbm, q_hbm, k_ref, v_ref, *refs):
    outs, edges = refs[:3], refs[3:5]
    score_ref, q_ref, lists_ref, crowded_ref = refs[5:9]
    own, pattern_ref, order_ref, rank_ref, sems, near_sems, sem = refs[9:]
    position, rep = lax.axis_index(("seq", "rep")), lax.axis_index("rep")
    width = k_ref.shape[1]
    held = Copies(near_sems)
    held.start(q_hbm, q_ref)
    held.start(k_ref, own)
    copies = Copies(sems)
    for edge, begin in zip(edges, ((blocks - 1) * BLOCK, 0)):
        for at, rows in enumerate((k_ref, v_ref)):
            copies.start(rows.at[pl.ds(begin, BLOCK), :], edge.at[:, pl.ds(at * width, width)])
    load(pattern_hbm, pattern_ref, sem)
    pack(pattern_ref, blocks, shards, caps, v_ref, outs, order_ref, copies)
    for at, ahead in enumerate((3, 4)):
        source = lax.rem(position + ahead, shards)
        bits = listed_bits(
            pattern_ref, blocks, shards, source, (rep == 0) if ahead == 4 else True
        )
        rank = jnp.int32(0)
        for b, bit in enumerate(bits):
            rank_ref[at, b] = rank if ahead == 4 else jnp.where(rep == 1, rank, b)
            rank = rank + bit
    for i in range(blocks):
        for slot in range(pattern_ref.shape[0]):
            entry = pattern_ref[slot, position * blocks + i]
            lists_ref[i, slot] = entry
            if slot >= 3:
                source = lax.rem(position + slot - 1, shards)
                at = jnp.where(entry >= 0, entry - source * blocks, 0)
                at = at if slot == 3 else rank_ref[slot - 4, at]
                lists_ref[i, pattern_ref.shape[0] + slot - 3] = at
    crowded = jnp.int32(0)
    for source in range(shards):
        count = sum(listed_bits(pattern_ref, blocks, shards, source, source % 2 == 0))
        crowded = jnp.maximum(crowded, jnp.where(count > caps[source % 2], 1, 0))
    crowded_ref[0] = crowded
    held.wait()
    for i in range(blocks):
        query = block_rows(q_ref, i)
        for slot, other in enumerate((i, i - 1, i + 1)):
            if 0 <= other < blocks:
                score_ref[i, slot] = score(query, block_rows(own, other))
    copies.wait()


def packed_shapes(blocks, caps, rows):
    sizes = (caps[0], caps[1], blocks - caps[1])
    return [jax.ShapeDtypeStruct((n * BLOCK, rows.shape[1]), rows.dtype) for n in sizes]


def pack_keys(blocks, shards, caps, columns, k):
    return pl.pallas_call(
        lambda *refs: key_kernel(blocks, shards, caps, *refs),
        out_shape=packed_shapes(blocks, caps, k),
        in_specs=[HBM] * 2,
        out_specs=[VMEM] * 3,
        scratch_shapes=[
            pltpu.SMEM(columns.shape, jnp.int32),
            pltpu.SMEM((blocks,), jnp.int32),
            pltpu.SemaphoreType.DMA((2 * blocks,)),
            pltpu.SemaphoreType.DMA,
        ],
    )(columns, k)


def plan(blocks, shards, caps, columns, q, k, v):
    width, list_len = k.shape[1], columns.shape[0]
    return pl.pallas_call(
        lambda *refs: plan_kernel(blocks, shards, caps, *refs),
        out_shape=packed_shapes(blocks, caps, v)
        + [jax.ShapeDtypeStruct((BLOCK, 2 * width), k.dtype)] * 2
        + [
            jax.ShapeDtypeStruct((blocks, 3, BLOCK, BLOCK), jnp.float32),
            jax.ShapeDtypeStruct(q.shape, q.dtype),
            jax.ShapeDtypeStruct((blocks, 2 * list_len - 3), jnp.int32),
            jax.ShapeDtypeStruct((1,), jnp.int32),
        ],
        in_specs=[HBM] * 4,
        out_specs=[VMEM] * 7 + [SMEM] * 2,
        scratch_shapes=[
            pltpu.VMEM(k.shape, k.dtype),
            pltpu.SMEM(columns.shape, jnp.int32),
            pltpu.SMEM((blocks,), jnp.int32),
            pltpu.SMEM((2, blocks), jnp.int32),
            pltpu.SemaphoreType.DMA((2 * blocks + 4,)),
            pltpu.SemaphoreType.DMA((2,)),
            pltpu.SemaphoreType.DMA,
        ],
        cost_estimate=pl.CostEstimate(flops=100663296, bytes_accessed=4194304, transcendentals=0),
        compiler_params=pltpu.CompilerParams(vmem_limit_bytes=LIMIT),
    )(columns, q, k, v)


class Whole:
    def __init__(self, caps, wide, slim, rest, whole, lists_hbm, lists_ref, sems):
        self.parts = (0, wide, caps[0] - caps[1]), (1, slim, 0)
        self.rest, self.whole, self.sem = rest, whole, sems.at[0]
        self.lists = pltpu.make_async_copy(lists_hbm, lists_ref, sems.at[1])

    def left(self, used, skip):
        count = self.whole.shape[0] - used
        return pltpu.make_async_copy(
            self.rest.at[pl.ds(skip * BLOCK, count), :], self.whole.at[pl.ds(used, count), :], self.sem
        )

    def on_core(self, act):
        for core, first, skip in self.parts:

            @pl.when(lax.axis_index("rep") == core)
            def _():
                act(first, skip)

    def start(self):
        self.lists.start()

        def begin(first, skip):
            self.left(first.shape[0], skip).start()
            self.whole[: first.shape[0], :] = first[...]

        self.on_core(begin)

    def wait(self):
        self.on_core(lambda first, skip: self.left(first.shape[0], skip).wait())


def present(scores, entry):
    return scores + jnp.where(entry >= 0, 0.0, -jnp.inf).astype(jnp.float32)


def score_kernel(
    blocks, caps, lists_hbm, q_ref, near_ref, low, high,
    near_far, other_far, wide, slim, rest, exp_ref, sums_ref, sent_ref,
    whole, lists_ref, sems,
):
    gathered = Whole(caps, wide, slim, rest, whole, lists_hbm, lists_ref, sems)
    gathered.start()
    near = near_ref.shape[1]
    sums_ref[...] = jnp.zeros_like(sums_ref)
    gathered.lists.wait()
    for i in range(blocks):
        query = block_rows(q_ref, i)
        for slot, key in enumerate(far_blocks(i, lists_ref, (near_far, other_far))):
            exp_ref[i, near + slot] = present(score(query, key), lists_ref[i, near + slot])
    gathered.wait()
    for i in range(blocks):
        query = block_rows(q_ref, i)
        scores = [near_ref[i, 0]]
        scores.append(score(query, low[...]) if i == 0 else near_ref[i, 1])
        scores.append(score(query, high[...]) if i == blocks - 1 else near_ref[i, 2])
        scores.extend([exp_ref[i, near], exp_ref[i, near + 1]])
        last = score(query, block_rows(whole, lists_ref[i, LISTED + 2]))
        scores.append(present(last, lists_ref[i, near + 2]))
        peak = scores[0]
        for part in scores[1:]:
            peak = jnp.maximum(peak, part)
        peak = jnp.max(peak, axis=1, keepdims=True)
        exps = [jnp.exp(part - peak) for part in scores]
        for slot, value in enumerate(exps):
            exp_ref[i, slot] = value
        scale = 1.0 / row_total(exps)
        add_columns(sums_ref, lists_ref, i, [value * scale for value in exps])
    sent_ref[...] = sums_ref[...].astype(sent_ref.dtype)


def scaled(exp_ref, lists_ref, i, factor_refs):
    parts = []
    for slot in range(exp_ref.shape[1]):
        value = exp_ref[i, slot]
        for factor in factor_refs:
            value = value * factor[pl.ds(jnp.maximum(lists_ref[i, slot], 0), 1), :]
        parts.append(value)
    return parts


def round_kernel(
    blocks, lists_hbm, exp_ref, sum_a, sum_b, factor_ref, sums_ref, sent_ref, lists_ref, sem
):
    load(lists_hbm, lists_ref, sem)
    factor_ref[...] = 1.0 / (sum_a[...] + sum_b[...].astype(jnp.float32))
    sums_ref[...] = jnp.zeros_like(sums_ref)
    for i in range(blocks):
        parts = scaled(exp_ref, lists_ref, i, [factor_ref])
        scale = 1.0 / row_total(parts)
        add_columns(sums_ref, lists_ref, i, [part * scale for part in parts])
    sent_ref[...] = sums_ref[...].astype(sent_ref.dtype)


def output_kernel(
    blocks, caps, lists_hbm, exp_ref, factor_ref, sum_a, sum_b, own, low, high,
    near_far, other_far, wide, slim, rest, out_ref, last_ref, whole, partial_ref, weight_ref,
    lists_ref, sems,
):
    gathered = Whole(caps, wide, slim, rest, whole, lists_hbm, lists_ref, sems)
    gathered.start()
    last_ref[...] = 1.0 / (sum_a[...] + sum_b[...].astype(jnp.float32))
    gathered.lists.wait()
    for i in range(blocks):
        parts = scaled(exp_ref, lists_ref, i, [factor_ref, last_ref])
        scale = 1.0 / row_total(parts)
        values = near_blocks(i, blocks, own, low, high)
        values += far_blocks(i, lists_ref, (near_far, other_far))
        parts = [(part * scale).astype(jnp.bfloat16) for part in parts]
        total = None
        for part, value in zip(parts, values):
            term = jnp.dot(part, value, preferred_element_type=jnp.float32)
            total = term if total is None else total + term
        partial_ref[i] = total
        weight_ref[i] = parts[-1]
    gathered.wait()
    for i in range(blocks):
        value = block_rows(whole, lists_ref[i, LISTED + 2])
        total = partial_ref[i] + jnp.dot(weight_ref[i], value, preferred_element_type=jnp.float32)
        out_ref[pl.ds(i * BLOCK, BLOCK), :] = total.astype(out_ref.dtype)


def shifted(x, axis, by):
    devices = lax.axis_size(axis)
    return lax.ppermute(x, axis, [(i, (i + by) % devices) for i in range(devices)])


def swapped(x):
    return lax.ppermute(x, "rep", [(0, 1), (1, 0)])


def over_seq(mine, sent):
    devices = lax.axis_size("seq")
    pairs = lambda by: [(i, i ^ by) for i in range(devices)]
    if devices <= 4:
        parts = [lax.ppermute(sent, "seq", pairs(by)) for by in reversed(range(1, devices))]
        return sum([part.astype(mine.dtype) for part in parts], mine)
    by = 1
    while by < devices:
        mine = mine + lax.ppermute(mine, "seq", pairs(by))
        by *= 2
    return mine


def two_away(wide, slim):
    chips = lax.axis_size("seq")
    moves = [(i, (i - 2) % chips) for i in range(chips)]
    axes = ("seq", "rep")
    return (
        lax.ppermute(wide, axes, [(2 * i, 2 * j) for i, j in moves]),
        lax.ppermute(slim, axes, [(2 * i + 1, 2 * j + 1) for i, j in moves]),
    )


def remainder(crowded, *rest):
    return lax.cond(
        crowded,
        lambda *x: tuple(shifted(part, "seq", -2) for part in x),
        lambda *x: x,
        *rest,
    )


def with_swap(near, wide, rest, caps, rep):
    beyond = jnp.concatenate([wide, rest[(caps[0] - caps[1]) * BLOCK :]], axis=0)
    return swapped(jnp.where(rep == 0, beyond, near))


def body(queries, key_rows, value_rows, pattern):
    tok_local, heads_local, width = queries.shape
    assert heads_local == 1
    blocks = tok_local // BLOCK
    list_len = pattern.shape[1]
    far_count = list_len - 3
    total_blocks = pattern.shape[0]
    axes = ("seq", "rep")
    shards = lax.axis_size(axes)
    rep = lax.axis_index("rep")
    q = queries.reshape(tok_local, width)
    k = key_rows.reshape(tok_local, width)
    v = value_rows.reshape(tok_local, width)

    caps = (blocks - blocks // 8, blocks - 3 * blocks // 8)
    columns = pattern.T
    k_near = shifted(k, "seq", -1)
    k_wide, k_slim, k_rest = pack_keys(blocks, shards, caps, columns, k)
    k_in, columns, k_wide, k_slim, k_rest = lax.optimization_barrier(
        (k, columns, k_wide, k_slim, k_rest)
    )
    *v_packs, edges_low, edges_high, near_scores, q_held, lists, crowded = plan(
        blocks, shards, caps, columns, q, k_in, v
    )
    v_wide, v_slim, v_rest = v_packs
    k_wide, k_slim = two_away(k_wide, k_slim)
    k_rest, v_rest = remainder(crowded[0] > 0, k_rest, v_rest)
    low = shifted(edges_low, axes, 1)
    high = shifted(edges_high, axes, -1)

    near_scores, v_in = lax.optimization_barrier((near_scores, v))
    v_near = shifted(v_in, "seq", -1)
    k_near, k_wide, k_slim = lax.optimization_barrier((k_near, k_wide, k_slim))
    k_other = with_swap(k_near, k_wide, k_rest, caps, rep)
    exps, sums, sent = pl.pallas_call(
        lambda *refs: score_kernel(blocks, caps, *refs),
        out_shape=(
            jax.ShapeDtypeStruct((blocks, list_len, BLOCK, BLOCK), jnp.float32),
            jax.ShapeDtypeStruct((total_blocks, BLOCK), jnp.float32),
            jax.ShapeDtypeStruct((total_blocks, BLOCK), SENT),
        ),
        in_specs=[HBM] + [VMEM] * 8 + [ANY],
        out_specs=(VMEM, VMEM, VMEM),
        scratch_shapes=[
            pltpu.VMEM((tok_local, width), jnp.bfloat16),
            pltpu.SMEM((blocks, 2 * list_len - 3), jnp.int32),
            pltpu.SemaphoreType.DMA((2,)),
        ],
        cost_estimate=pl.CostEstimate(flops=100663296, bytes_accessed=6291456, transcendentals=786432),
        compiler_params=pltpu.CompilerParams(vmem_limit_bytes=LIMIT),
    )(
        lists, q_held, near_scores, low[:, :width], high[:, :width],
        k_near, k_other, k_wide, k_slim, k_rest,
    )

    v_wide, v_slim, sent = lax.optimization_barrier((v_wide, v_slim, sent))
    mine = over_seq(sums, sent)
    v_wide, v_slim = two_away(v_wide, v_slim)
    mine, v_near = lax.optimization_barrier((mine, v_near))
    v_wide, v_slim = lax.optimization_barrier((v_wide, v_slim))
    v_other = with_swap(v_near, v_wide, v_rest, caps, rep)
    factor, sums, sent = pl.pallas_call(
        lambda *refs: round_kernel(blocks, *refs),
        out_shape=(
            jax.ShapeDtypeStruct((total_blocks, BLOCK), jnp.float32),
            jax.ShapeDtypeStruct((total_blocks, BLOCK), jnp.float32),
            jax.ShapeDtypeStruct((total_blocks, BLOCK), SENT),
        ),
        in_specs=[HBM] + [VMEM] * 3,
        out_specs=(VMEM, VMEM, VMEM),
        scratch_shapes=[
            pltpu.SMEM((blocks, 2 * list_len - 3), jnp.int32),
            pltpu.SemaphoreType.DMA,
        ],
        cost_estimate=pl.CostEstimate(flops=7864320, bytes_accessed=4194304, transcendentals=0),
        compiler_params=pltpu.CompilerParams(vmem_limit_bytes=LIMIT),
    )(lists, exps, mine, swapped(mine.astype(SENT)))

    mine = over_seq(sums, sent)
    out = pl.pallas_call(
        lambda *refs: output_kernel(blocks, caps, *refs),
        out_shape=jax.ShapeDtypeStruct((tok_local, width), jnp.bfloat16),
        in_specs=[HBM] + [VMEM] * 11 + [ANY],
        out_specs=VMEM,
        scratch_shapes=[
            pltpu.VMEM((total_blocks, BLOCK), jnp.float32),
            pltpu.VMEM((tok_local, width), jnp.bfloat16),
            pltpu.VMEM((blocks, BLOCK, width), jnp.float32),
            pltpu.VMEM((blocks, BLOCK, BLOCK), jnp.bfloat16),
            pltpu.SMEM((blocks, 2 * list_len - 3), jnp.int32),
            pltpu.SemaphoreType.DMA((2,)),
        ],
        cost_estimate=pl.CostEstimate(flops=201326592, bytes_accessed=6291456, transcendentals=0),
        compiler_params=pltpu.CompilerParams(vmem_limit_bytes=LIMIT),
    )(
        lists, exps, factor, mine, swapped(mine.astype(SENT)), v, low[:, width:], high[:, width:],
        v_near, v_other, v_wide, v_slim, v_rest,
    )
    return out.reshape(tok_local, heads_local, width)


def solution(mesh):
    in_specs = (
        P(("groups", "seq", "rep"), "head", None),
        P(("groups", "seq", "rep"), "head", None),
        P(("groups", "seq", "rep"), "head", None),
        P("groups", None),
    )
    out_specs = P(("groups", "seq", "rep"), "head", None)
    return jax.shard_map(body, mesh=mesh, in_specs=in_specs, out_specs=out_specs, check_vma=False)
```

```python
import math

import jax
import jax.numpy as jnp
from jax import lax
from jax.experimental import pallas as pl
from jax.experimental.pallas import tpu as pltpu
from jax.sharding import PartitionSpec as P

BLOCK = 128
ITERS = 2
LISTED = 6
SENT = jnp.bfloat16
VMEM = pl.BlockSpec(memory_space=pltpu.VMEM)
ANY = pl.BlockSpec(memory_space=pl.ANY)
HBM = pl.BlockSpec(memory_space=pltpu.HBM)
SMEM = pl.BlockSpec(memory_space=pltpu.SMEM)
LIMIT = 32 * 1024 * 1024


def block_rows(ref, index):
    start = index * BLOCK
    if not isinstance(index, int):
        start = pl.multiple_of(start, BLOCK)
    return ref[pl.ds(start, BLOCK), :]


def near_blocks(i, blocks, own, low, high):
    before = low[...] if i == 0 else block_rows(own, i - 1)
    after = high[...] if i == blocks - 1 else block_rows(own, i + 1)
    return [block_rows(own, i), before, after]


def far_blocks(i, lists_ref, fars):
    return [block_rows(far, lists_ref[i, LISTED + slot]) for slot, far in enumerate(fars)]


def score(query, key):
    product = lax.dot_general(
        query, key, (((1,), (1,)), ((), ())), preferred_element_type=jnp.float32
    )
    return product * (1.0 / math.sqrt(key.shape[1]))


def add_columns(sums_ref, lists_ref, i, weights):
    for slot, weight in enumerate(weights):
        at = pl.ds(jnp.maximum(lists_ref[i, slot], 0), 1)
        sums_ref[at, :] += jnp.sum(weight, axis=0, keepdims=True)


def row_total(parts):
    total = parts[0]
    for part in parts[1:]:
        total = total + part
    return jnp.sum(total, axis=1, keepdims=True)


def listed_bits(pattern_ref, blocks, shards, source, first_core):
    wanted = jnp.int32(0)
    for back, column, counted in ((4, 5, True), (3, 4, first_core)):
        if counted is False:
            continue
        first = (source + shards - back) % shards * blocks
        for i in range(blocks):
            entry = pattern_ref[column, first + i]
            bit = jnp.left_shift(jnp.int32(1), jnp.maximum(entry - source * blocks, 0))
            hit = entry >= 0 if counted is True else (entry >= 0) & counted
            wanted = jnp.where(hit, wanted | bit, wanted)
    return [jnp.bitwise_and(jnp.right_shift(wanted, b), 1) for b in range(blocks)]


class Copies:
    def __init__(self, sems):
        self.sems, self.started = sems, []

    def start(self, source, target):
        copy = pltpu.make_async_copy(source, target, self.sems.at[len(self.started)])
        copy.start()
        self.started.append(copy)

    def wait(self):
        for copy in self.started:
            copy.wait()


def pack(pattern_ref, blocks, shards, caps, rows, outs, order_ref, copies):
    position, rep = lax.axis_index(("seq", "rep")), lax.axis_index("rep")
    bits = listed_bits(pattern_ref, blocks, shards, position, rep == 0)
    rank, spare = jnp.int32(0), sum(bits)
    for b, bit in enumerate(bits):
        order_ref[jnp.where(bit == 1, rank, spare)] = b
        rank, spare = rank + bit, spare + 1 - bit
    for out, first in zip(outs, (0, 0, caps[1])):
        for t in range(out.shape[0] // BLOCK):
            begin = pl.multiple_of(order_ref[first + t] * BLOCK, BLOCK)
            copies.start(rows.at[pl.ds(begin, BLOCK), :], out.at[pl.ds(t * BLOCK, BLOCK), :])


def load(source, target, sem):
    copy = pltpu.make_async_copy(source, target, sem)
    copy.start()
    copy.wait()


def key_kernel(blocks, shards, caps, pattern_hbm, k_ref, *refs):
    outs, (pattern_ref, order_ref, sems, sem) = refs[:3], refs[3:]
    load(pattern_hbm, pattern_ref, sem)
    copies = Copies(sems)
    pack(pattern_ref, blocks, shards, caps, k_ref, outs, order_ref, copies)
    copies.wait()


def plan_kernel(blocks, shards, caps, pattern_hbm, q_hbm, k_ref, v_ref, *refs):
    outs, edges = refs[:3], refs[3:5]
    score_ref, q_ref, lists_ref, excess_ref = refs[5:9]
    own, pattern_ref, order_ref, rank_ref, sems, near_sems, sem = refs[9:]
    position, rep = lax.axis_index(("seq", "rep")), lax.axis_index("rep")
    width = k_ref.shape[1]
    held = Copies(near_sems)
    held.start(q_hbm, q_ref)
    held.start(k_ref, own)
    copies = Copies(sems)
    for edge, begin in zip(edges, ((blocks - 1) * BLOCK, 0)):
        for at, rows in enumerate((k_ref, v_ref)):
            copies.start(rows.at[pl.ds(begin, BLOCK), :], edge.at[:, pl.ds(at * width, width)])
    load(pattern_hbm, pattern_ref, sem)
    pack(pattern_ref, blocks, shards, caps, v_ref, outs, order_ref, copies)
    for at, ahead in enumerate((3, 4)):
        source = lax.rem(position + ahead, shards)
        bits = listed_bits(
            pattern_ref, blocks, shards, source, (rep == 0) if ahead == 4 else True
        )
        rank = jnp.int32(0)
        for b, bit in enumerate(bits):
            rank_ref[at, b] = rank if ahead == 4 else jnp.where(rep == 1, rank, b)
            rank = rank + bit
    for i in range(blocks):
        for slot in range(pattern_ref.shape[0]):
            entry = pattern_ref[slot, position * blocks + i]
            lists_ref[i, slot] = entry
            if slot >= 3:
                source = lax.rem(position + slot - 1, shards)
                at = jnp.where(entry >= 0, entry - source * blocks, 0)
                at = at if slot == 3 else rank_ref[slot - 4, at]
                lists_ref[i, pattern_ref.shape[0] + slot - 3] = at
    excess = jnp.int32(0)
    for source in range(shards):
        count = sum(listed_bits(pattern_ref, blocks, shards, source, source % 2 == 0))
        excess = jnp.maximum(excess, jnp.minimum(count - caps[source % 2], 2))
    excess_ref[0] = excess
    held.wait()
    for i in range(blocks):
        query = block_rows(q_ref, i)
        for slot, other in enumerate((i, i - 1, i + 1)):
            if 0 <= other < blocks:
                score_ref[i, slot] = score(query, block_rows(own, other))
    copies.wait()


def packed_shapes(blocks, caps, rows):
    sizes = (caps[0], caps[1], blocks - caps[1])
    return [jax.ShapeDtypeStruct((n * BLOCK, rows.shape[1]), rows.dtype) for n in sizes]


def pack_keys(blocks, shards, caps, columns, k):
    return pl.pallas_call(
        lambda *refs: key_kernel(blocks, shards, caps, *refs),
        out_shape=packed_shapes(blocks, caps, k),
        in_specs=[HBM] * 2,
        out_specs=[VMEM] * 3,
        scratch_shapes=[
            pltpu.SMEM(columns.shape, jnp.int32),
            pltpu.SMEM((blocks,), jnp.int32),
            pltpu.SemaphoreType.DMA((2 * blocks,)),
            pltpu.SemaphoreType.DMA,
        ],
    )(columns, k)


def plan(blocks, shards, caps, columns, q, k, v):
    width, list_len = k.shape[1], columns.shape[0]
    return pl.pallas_call(
        lambda *refs: plan_kernel(blocks, shards, caps, *refs),
        out_shape=packed_shapes(blocks, caps, v)
        + [jax.ShapeDtypeStruct((BLOCK, 2 * width), k.dtype)] * 2
        + [
            jax.ShapeDtypeStruct((blocks, 3, BLOCK, BLOCK), jnp.float32),
            jax.ShapeDtypeStruct(q.shape, q.dtype),
            jax.ShapeDtypeStruct((blocks, 2 * list_len - 3), jnp.int32),
            jax.ShapeDtypeStruct((1,), jnp.int32),
        ],
        in_specs=[HBM] * 4,
        out_specs=[VMEM] * 7 + [SMEM] * 2,
        scratch_shapes=[
            pltpu.VMEM(k.shape, k.dtype),
            pltpu.SMEM(columns.shape, jnp.int32),
            pltpu.SMEM((blocks,), jnp.int32),
            pltpu.SMEM((2, blocks), jnp.int32),
            pltpu.SemaphoreType.DMA((2 * blocks + 4,)),
            pltpu.SemaphoreType.DMA((2,)),
            pltpu.SemaphoreType.DMA,
        ],
        cost_estimate=pl.CostEstimate(flops=100663296, bytes_accessed=4194304, transcendentals=0),
        compiler_params=pltpu.CompilerParams(vmem_limit_bytes=LIMIT),
    )(columns, q, k, v)


class Whole:
    def __init__(self, caps, wide, slim, rest, whole, lists_hbm, lists_ref, sems):
        self.parts = (0, wide, caps[0] - caps[1]), (1, slim, 0)
        self.rest, self.whole, self.sem = rest, whole, sems.at[0]
        self.lists = pltpu.make_async_copy(lists_hbm, lists_ref, sems.at[1])

    def left(self, used, skip):
        count = self.whole.shape[0] - used
        return pltpu.make_async_copy(
            self.rest.at[pl.ds(skip * BLOCK, count), :], self.whole.at[pl.ds(used, count), :], self.sem
        )

    def on_core(self, act):
        for core, first, skip in self.parts:

            @pl.when(lax.axis_index("rep") == core)
            def _():
                act(first, skip)

    def start(self):
        self.lists.start()

        def begin(first, skip):
            self.left(first.shape[0], skip).start()
            self.whole[: first.shape[0], :] = first[...]

        self.on_core(begin)

    def wait(self):
        self.on_core(lambda first, skip: self.left(first.shape[0], skip).wait())


def present(scores, entry):
    return scores + jnp.where(entry >= 0, 0.0, -jnp.inf).astype(jnp.float32)


def score_kernel(
    blocks, caps, lists_hbm, q_ref, near_ref, low, high,
    near_far, other_far, wide, slim, rest, exp_ref, sums_ref, sent_ref,
    whole, lists_ref, sems,
):
    gathered = Whole(caps, wide, slim, rest, whole, lists_hbm, lists_ref, sems)
    gathered.start()
    near = near_ref.shape[1]
    sums_ref[...] = jnp.zeros_like(sums_ref)
    gathered.lists.wait()
    for i in range(blocks):
        query = block_rows(q_ref, i)
        for slot, key in enumerate(far_blocks(i, lists_ref, (near_far, other_far))):
            exp_ref[i, near + slot] = present(score(query, key), lists_ref[i, near + slot])
    gathered.wait()
    for i in range(blocks):
        query = block_rows(q_ref, i)
        scores = [near_ref[i, 0]]
        scores.append(score(query, low[...]) if i == 0 else near_ref[i, 1])
        scores.append(score(query, high[...]) if i == blocks - 1 else near_ref[i, 2])
        scores.extend([exp_ref[i, near], exp_ref[i, near + 1]])
        last = score(query, block_rows(whole, lists_ref[i, LISTED + 2]))
        scores.append(present(last, lists_ref[i, near + 2]))
        peak = scores[0]
        for part in scores[1:]:
            peak = jnp.maximum(peak, part)
        peak = jnp.max(peak, axis=1, keepdims=True)
        exps = [jnp.exp(part - peak) for part in scores]
        for slot, value in enumerate(exps):
            exp_ref[i, slot] = value
        scale = 1.0 / row_total(exps)
        add_columns(sums_ref, lists_ref, i, [value * scale for value in exps])
    sent_ref[...] = sums_ref[...].astype(sent_ref.dtype)


def scaled(exp_ref, lists_ref, i, factor_refs):
    parts = []
    for slot in range(exp_ref.shape[1]):
        value = exp_ref[i, slot]
        for factor in factor_refs:
            value = value * factor[pl.ds(jnp.maximum(lists_ref[i, slot], 0), 1), :]
        parts.append(value)
    return parts


def round_kernel(
    blocks, lists_hbm, exp_ref, sum_a, sum_b, factor_ref, sums_ref, sent_ref, lists_ref, sem
):
    load(lists_hbm, lists_ref, sem)
    factor_ref[...] = 1.0 / (sum_a[...] + sum_b[...].astype(jnp.float32))
    sums_ref[...] = jnp.zeros_like(sums_ref)
    for i in range(blocks):
        parts = scaled(exp_ref, lists_ref, i, [factor_ref])
        scale = 1.0 / row_total(parts)
        add_columns(sums_ref, lists_ref, i, [part * scale for part in parts])
    sent_ref[...] = sums_ref[...].astype(sent_ref.dtype)


def output_kernel(
    blocks, caps, lists_hbm, exp_ref, factor_ref, sum_a, sum_b, own, low, high,
    near_far, other_far, wide, slim, rest, out_ref, last_ref, whole, partial_ref, weight_ref,
    lists_ref, sems,
):
    gathered = Whole(caps, wide, slim, rest, whole, lists_hbm, lists_ref, sems)
    gathered.start()
    last_ref[...] = 1.0 / (sum_a[...] + sum_b[...].astype(jnp.float32))
    gathered.lists.wait()
    for i in range(blocks):
        parts = scaled(exp_ref, lists_ref, i, [factor_ref, last_ref])
        scale = 1.0 / row_total(parts)
        values = near_blocks(i, blocks, own, low, high)
        values += far_blocks(i, lists_ref, (near_far, other_far))
        parts = [(part * scale).astype(jnp.bfloat16) for part in parts]
        total = None
        for part, value in zip(parts, values):
            term = jnp.dot(part, value, preferred_element_type=jnp.float32)
            total = term if total is None else total + term
        partial_ref[i] = total
        weight_ref[i] = parts[-1]
    gathered.wait()
    for i in range(blocks):
        value = block_rows(whole, lists_ref[i, LISTED + 2])
        total = partial_ref[i] + jnp.dot(weight_ref[i], value, preferred_element_type=jnp.float32)
        out_ref[pl.ds(i * BLOCK, BLOCK), :] = total.astype(out_ref.dtype)


def shifted(x, axis, by):
    devices = lax.axis_size(axis)
    return lax.ppermute(x, axis, [(i, (i + by) % devices) for i in range(devices)])


def swapped(x):
    return lax.ppermute(x, "rep", [(0, 1), (1, 0)])


def over_seq(mine, sent):
    devices = lax.axis_size("seq")
    pairs = lambda by: [(i, i ^ by) for i in range(devices)]
    if devices <= 4:
        parts = [lax.ppermute(sent, "seq", pairs(by)) for by in reversed(range(1, devices))]
        return sum([part.astype(mine.dtype) for part in parts], mine)
    by = 1
    while by < devices:
        mine = mine + lax.ppermute(mine, "seq", pairs(by))
        by *= 2
    return mine


def two_away(wide, slim):
    chips = lax.axis_size("seq")
    moves = [(i, (i - 2) % chips) for i in range(chips)]
    axes = ("seq", "rep")
    return (
        lax.ppermute(wide, axes, [(2 * i, 2 * j) for i, j in moves]),
        lax.ppermute(slim, axes, [(2 * i + 1, 2 * j + 1) for i, j in moves]),
    )


def remainder(excess, caps, rep, *rest):
    def first(*parts):
        at = jnp.where(rep == 0, (caps[0] - caps[1]) * BLOCK, 0)
        sent = [lax.dynamic_slice_in_dim(part, at, BLOCK, 0) for part in parts]
        sent = [shifted(part, "seq", -2) for part in sent]
        return tuple(
            lax.dynamic_update_slice_in_dim(part, new, at, 0) for part, new in zip(parts, sent)
        )

    return lax.switch(
        excess,
        (
            lambda *parts: parts,
            first,
            lambda *parts: tuple(shifted(part, "seq", -2) for part in parts),
        ),
        *rest,
    )


def with_swap(near, wide, rest, caps, rep):
    beyond = jnp.concatenate([wide, rest[(caps[0] - caps[1]) * BLOCK :]], axis=0)
    return swapped(jnp.where(rep == 0, beyond, near))


def body(queries, key_rows, value_rows, pattern):
    tok_local, heads_local, width = queries.shape
    assert heads_local == 1
    blocks = tok_local // BLOCK
    list_len = pattern.shape[1]
    far_count = list_len - 3
    total_blocks = pattern.shape[0]
    axes = ("seq", "rep")
    shards = lax.axis_size(axes)
    rep = lax.axis_index("rep")
    q = queries.reshape(tok_local, width)
    k = key_rows.reshape(tok_local, width)
    v = value_rows.reshape(tok_local, width)

    caps = (blocks - blocks // 8, blocks - blocks // 2)
    columns = pattern.T
    k_near = shifted(k, "seq", -1)
    k_wide, k_slim, k_rest = pack_keys(blocks, shards, caps, columns, k)
    k_in, columns, k_wide, k_slim, k_rest = lax.optimization_barrier(
        (k, columns, k_wide, k_slim, k_rest)
    )
    *v_packs, edges_low, edges_high, near_scores, q_held, lists, excess = plan(
        blocks, shards, caps, columns, q, k_in, v
    )
    v_wide, v_slim, v_rest = v_packs
    k_wide, k_slim = two_away(k_wide, k_slim)
    k_rest, v_rest = remainder(excess[0], caps, rep, k_rest, v_rest)
    low = shifted(edges_low, axes, 1)
    high = shifted(edges_high, axes, -1)

    near_scores, v_in = lax.optimization_barrier((near_scores, v))
    v_near = shifted(v_in, "seq", -1)
    k_near, k_wide, k_slim = lax.optimization_barrier((k_near, k_wide, k_slim))
    k_other = with_swap(k_near, k_wide, k_rest, caps, rep)
    exps, sums, sent = pl.pallas_call(
        lambda *refs: score_kernel(blocks, caps, *refs),
        out_shape=(
            jax.ShapeDtypeStruct((blocks, list_len, BLOCK, BLOCK), jnp.float32),
            jax.ShapeDtypeStruct((total_blocks, BLOCK), jnp.float32),
            jax.ShapeDtypeStruct((total_blocks, BLOCK), SENT),
        ),
        in_specs=[HBM] + [VMEM] * 8 + [ANY],
        out_specs=(VMEM, VMEM, VMEM),
        scratch_shapes=[
            pltpu.VMEM((tok_local, width), jnp.bfloat16),
            pltpu.SMEM((blocks, 2 * list_len - 3), jnp.int32),
            pltpu.SemaphoreType.DMA((2,)),
        ],
        cost_estimate=pl.CostEstimate(flops=100663296, bytes_accessed=6291456, transcendentals=786432),
        compiler_params=pltpu.CompilerParams(vmem_limit_bytes=LIMIT),
    )(
        lists, q_held, near_scores, low[:, :width], high[:, :width],
        k_near, k_other, k_wide, k_slim, k_rest,
    )

    v_wide, v_slim, sent = lax.optimization_barrier((v_wide, v_slim, sent))
    mine = over_seq(sums, sent)
    v_wide, v_slim = two_away(v_wide, v_slim)
    mine, v_near = lax.optimization_barrier((mine, v_near))
    v_wide, v_slim = lax.optimization_barrier((v_wide, v_slim))
    factor, sums, sent = pl.pallas_call(
        lambda *refs: round_kernel(blocks, *refs),
        out_shape=(
            jax.ShapeDtypeStruct((total_blocks, BLOCK), jnp.float32),
            jax.ShapeDtypeStruct((total_blocks, BLOCK), jnp.float32),
            jax.ShapeDtypeStruct((total_blocks, BLOCK), SENT),
        ),
        in_specs=[HBM] + [VMEM] * 3,
        out_specs=(VMEM, VMEM, VMEM),
        scratch_shapes=[
            pltpu.SMEM((blocks, 2 * list_len - 3), jnp.int32),
            pltpu.SemaphoreType.DMA,
        ],
        cost_estimate=pl.CostEstimate(flops=7864320, bytes_accessed=4194304, transcendentals=0),
        compiler_params=pltpu.CompilerParams(vmem_limit_bytes=LIMIT),
    )(lists, exps, mine, swapped(mine))

    v_far, factor = lax.optimization_barrier(((v_near, v_wide, v_rest), factor))
    v_near, v_wide, v_rest = v_far
    v_other = with_swap(v_near, v_wide, v_rest, caps, rep)
    mine = over_seq(sums, sent)
    out = pl.pallas_call(
        lambda *refs: output_kernel(blocks, caps, *refs),
        out_shape=jax.ShapeDtypeStruct((tok_local, width), jnp.bfloat16),
        in_specs=[HBM] + [VMEM] * 11 + [ANY],
        out_specs=VMEM,
        scratch_shapes=[
            pltpu.VMEM((total_blocks, BLOCK), jnp.float32),
            pltpu.VMEM((tok_local, width), jnp.bfloat16),
            pltpu.VMEM((blocks, BLOCK, width), jnp.float32),
            pltpu.VMEM((blocks, BLOCK, BLOCK), jnp.bfloat16),
            pltpu.SMEM((blocks, 2 * list_len - 3), jnp.int32),
            pltpu.SemaphoreType.DMA((2,)),
        ],
        cost_estimate=pl.CostEstimate(flops=201326592, bytes_accessed=6291456, transcendentals=0),
        compiler_params=pltpu.CompilerParams(vmem_limit_bytes=LIMIT),
    )(
        lists, exps, factor, mine, swapped(mine), v, low[:, width:], high[:, width:],
        v_near, v_other, v_wide, v_slim, v_rest,
    )
    return out.reshape(tok_local, heads_local, width)


def solution(mesh):
    in_specs = (
        P(("groups", "seq", "rep"), "head", None),
        P(("groups", "seq", "rep"), "head", None),
        P(("groups", "seq", "rep"), "head", None),
        P("groups", None),
    )
    out_specs = P(("groups", "seq", "rep"), "head", None)
    return jax.shard_map(body, mesh=mesh, in_specs=in_specs, out_specs=out_specs, check_vma=False)
```

```python
import math

import jax
import jax.numpy as jnp
from jax import lax
from jax.experimental import pallas as pl
from jax.experimental.pallas import tpu as pltpu
from jax.sharding import PartitionSpec as P

BLOCK = 128
ITERS = 2
LISTED = 6
SENT = jnp.bfloat16
VMEM = pl.BlockSpec(memory_space=pltpu.VMEM)
ANY = pl.BlockSpec(memory_space=pl.ANY)
HBM = pl.BlockSpec(memory_space=pltpu.HBM)
SMEM = pl.BlockSpec(memory_space=pltpu.SMEM)
LIMIT = 32 * 1024 * 1024


def block_rows(ref, index):
    start = index * BLOCK
    if not isinstance(index, int):
        start = pl.multiple_of(start, BLOCK)
    return ref[pl.ds(start, BLOCK), :]


def near_blocks(i, blocks, own, low, high):
    before = low[...] if i == 0 else block_rows(own, i - 1)
    after = high[...] if i == blocks - 1 else block_rows(own, i + 1)
    return [block_rows(own, i), before, after]


def far_blocks(i, lists_ref, fars):
    return [block_rows(far, lists_ref[i, LISTED + slot]) for slot, far in enumerate(fars)]


def score(query, key):
    product = lax.dot_general(
        query, key, (((1,), (1,)), ((), ())), preferred_element_type=jnp.float32
    )
    return product * (1.0 / math.sqrt(key.shape[1]))


def add_columns(sums_ref, lists_ref, i, weights):
    for slot, weight in enumerate(weights):
        at = pl.ds(jnp.maximum(lists_ref[i, slot], 0), 1)
        sums_ref[at, :] += jnp.sum(weight, axis=0, keepdims=True)


def row_total(parts):
    total = parts[0]
    for part in parts[1:]:
        total = total + part
    return jnp.sum(total, axis=1, keepdims=True)


def listed_bits(pattern_ref, blocks, shards, source, first_core):
    wanted = jnp.int32(0)
    for back, column, counted in ((4, 5, True), (3, 4, first_core)):
        if counted is False:
            continue
        first = (source + shards - back) % shards * blocks
        for i in range(blocks):
            entry = pattern_ref[column, first + i]
            bit = jnp.left_shift(jnp.int32(1), jnp.maximum(entry - source * blocks, 0))
            hit = entry >= 0 if counted is True else (entry >= 0) & counted
            wanted = jnp.where(hit, wanted | bit, wanted)
    return [jnp.bitwise_and(jnp.right_shift(wanted, b), 1) for b in range(blocks)]


class Copies:
    def __init__(self, sems):
        self.sems, self.started = sems, []

    def start(self, source, target):
        copy = pltpu.make_async_copy(source, target, self.sems.at[len(self.started)])
        copy.start()
        self.started.append(copy)

    def wait(self):
        for copy in self.started:
            copy.wait()


def pack(pattern_ref, blocks, shards, caps, rows, outs, order_ref, copies):
    position, rep = lax.axis_index(("seq", "rep")), lax.axis_index("rep")
    bits = listed_bits(pattern_ref, blocks, shards, position, rep == 0)
    rank, spare = jnp.int32(0), sum(bits)
    for b, bit in enumerate(bits):
        order_ref[jnp.where(bit == 1, rank, spare)] = b
        rank, spare = rank + bit, spare + 1 - bit
    for out, first in zip(outs, (0, 0, caps[1])):
        for t in range(out.shape[0] // BLOCK):
            begin = pl.multiple_of(order_ref[first + t] * BLOCK, BLOCK)
            copies.start(rows.at[pl.ds(begin, BLOCK), :], out.at[pl.ds(t * BLOCK, BLOCK), :])


def load(source, target, sem):
    copy = pltpu.make_async_copy(source, target, sem)
    copy.start()
    copy.wait()


def key_kernel(blocks, shards, caps, pattern_hbm, k_ref, *refs):
    outs, (pattern_ref, order_ref, sems, sem) = refs[:3], refs[3:]
    load(pattern_hbm, pattern_ref, sem)
    copies = Copies(sems)
    pack(pattern_ref, blocks, shards, caps, k_ref, outs, order_ref, copies)
    copies.wait()


def plan_kernel(blocks, shards, caps, pattern_hbm, q_hbm, k_ref, v_ref, *refs):
    outs, edges = refs[:3], refs[3:5]
    score_ref, q_ref, lists_ref, crowded_ref = refs[5:9]
    own, pattern_ref, order_ref, rank_ref, sems, near_sems, sem = refs[9:]
    position, rep = lax.axis_index(("seq", "rep")), lax.axis_index("rep")
    width = k_ref.shape[1]
    held = Copies(near_sems)
    held.start(q_hbm, q_ref)
    held.start(k_ref, own)
    copies = Copies(sems)
    for edge, begin in zip(edges, ((blocks - 1) * BLOCK, 0)):
        for at, rows in enumerate((k_ref, v_ref)):
            copies.start(rows.at[pl.ds(begin, BLOCK), :], edge.at[:, pl.ds(at * width, width)])
    load(pattern_hbm, pattern_ref, sem)
    pack(pattern_ref, blocks, shards, caps, v_ref, outs, order_ref, copies)
    for at, ahead in enumerate((3, 4)):
        source = lax.rem(position + ahead, shards)
        bits = listed_bits(
            pattern_ref, blocks, shards, source, (rep == 0) if ahead == 4 else True
        )
        rank = jnp.int32(0)
        for b, bit in enumerate(bits):
            rank_ref[at, b] = rank if ahead == 4 else jnp.where(rep == 1, rank, b)
            rank = rank + bit
    for i in range(blocks):
        for slot in range(pattern_ref.shape[0]):
            entry = pattern_ref[slot, position * blocks + i]
            lists_ref[i, slot] = entry
            if slot >= 3:
                source = lax.rem(position + slot - 1, shards)
                at = jnp.where(entry >= 0, entry - source * blocks, 0)
                at = at if slot == 3 else rank_ref[slot - 4, at]
                lists_ref[i, pattern_ref.shape[0] + slot - 3] = at
    crowded = jnp.int32(0)
    for source in range(shards):
        count = sum(listed_bits(pattern_ref, blocks, shards, source, source % 2 == 0))
        crowded = jnp.maximum(crowded, jnp.where(count > caps[source % 2], 1, 0))
    crowded_ref[0] = crowded
    held.wait()
    for i in range(blocks):
        query = block_rows(q_ref, i)
        for slot, other in enumerate((i, i - 1, i + 1)):
            if 0 <= other < blocks:
                score_ref[i, slot] = score(query, block_rows(own, other))
    copies.wait()


def packed_shapes(blocks, caps, rows):
    sizes = (caps[0], caps[1], blocks - caps[1])
    return [jax.ShapeDtypeStruct((n * BLOCK, rows.shape[1]), rows.dtype) for n in sizes]


def pack_keys(blocks, shards, caps, columns, k):
    return pl.pallas_call(
        lambda *refs: key_kernel(blocks, shards, caps, *refs),
        out_shape=packed_shapes(blocks, caps, k),
        in_specs=[HBM] * 2,
        out_specs=[VMEM] * 3,
        scratch_shapes=[
            pltpu.SMEM(columns.shape, jnp.int32),
            pltpu.SMEM((blocks,), jnp.int32),
            pltpu.SemaphoreType.DMA((2 * blocks,)),
            pltpu.SemaphoreType.DMA,
        ],
    )(columns, k)


def plan(blocks, shards, caps, columns, q, k, v):
    width, list_len = k.shape[1], columns.shape[0]
    return pl.pallas_call(
        lambda *refs: plan_kernel(blocks, shards, caps, *refs),
        out_shape=packed_shapes(blocks, caps, v)
        + [jax.ShapeDtypeStruct((BLOCK, 2 * width), k.dtype)] * 2
        + [
            jax.ShapeDtypeStruct((blocks, 3, BLOCK, BLOCK), jnp.float32),
            jax.ShapeDtypeStruct(q.shape, q.dtype),
            jax.ShapeDtypeStruct((blocks, 2 * list_len - 3), jnp.int32),
            jax.ShapeDtypeStruct((1,), jnp.int32),
        ],
        in_specs=[HBM] * 4,
        out_specs=[VMEM] * 7 + [SMEM] * 2,
        scratch_shapes=[
            pltpu.VMEM(k.shape, k.dtype),
            pltpu.SMEM(columns.shape, jnp.int32),
            pltpu.SMEM((blocks,), jnp.int32),
            pltpu.SMEM((2, blocks), jnp.int32),
            pltpu.SemaphoreType.DMA((2 * blocks + 4,)),
            pltpu.SemaphoreType.DMA((2,)),
            pltpu.SemaphoreType.DMA,
        ],
        cost_estimate=pl.CostEstimate(flops=100663296, bytes_accessed=4194304, transcendentals=0),
        compiler_params=pltpu.CompilerParams(vmem_limit_bytes=LIMIT),
    )(columns, q, k, v)


class Whole:
    def __init__(self, caps, wide, slim, rest, whole, lists_hbm, lists_ref, sems):
        self.parts = (0, wide, caps[0] - caps[1]), (1, slim, 0)
        self.rest, self.whole, self.sem = rest, whole, sems.at[0]
        self.lists = pltpu.make_async_copy(lists_hbm, lists_ref, sems.at[1])

    def left(self, used, skip):
        count = self.whole.shape[0] - used
        return pltpu.make_async_copy(
            self.rest.at[pl.ds(skip * BLOCK, count), :], self.whole.at[pl.ds(used, count), :], self.sem
        )

    def on_core(self, act):
        for core, first, skip in self.parts:

            @pl.when(lax.axis_index("rep") == core)
            def _():
                act(first, skip)

    def start(self):
        self.lists.start()

        def begin(first, skip):
            self.left(first.shape[0], skip).start()
            self.whole[: first.shape[0], :] = first[...]

        self.on_core(begin)

    def wait(self):
        self.on_core(lambda first, skip: self.left(first.shape[0], skip).wait())


def present(scores, entry):
    return scores + jnp.where(entry >= 0, 0.0, -jnp.inf).astype(jnp.float32)


def score_kernel(
    blocks, caps, lists_hbm, q_ref, near_ref, low, high,
    near_far, other_far, wide, slim, rest, exp_ref, sums_ref, sent_ref,
    whole, lists_ref, sems,
):
    gathered = Whole(caps, wide, slim, rest, whole, lists_hbm, lists_ref, sems)
    gathered.start()
    near = near_ref.shape[1]
    sums_ref[...] = jnp.zeros_like(sums_ref)
    gathered.lists.wait()
    for i in range(blocks):
        query = block_rows(q_ref, i)
        for slot, key in enumerate(far_blocks(i, lists_ref, (near_far, other_far))):
            exp_ref[i, near + slot] = present(score(query, key), lists_ref[i, near + slot])
    gathered.wait()
    for i in range(blocks):
        query = block_rows(q_ref, i)
        scores = [near_ref[i, 0]]
        scores.append(score(query, low[...]) if i == 0 else near_ref[i, 1])
        scores.append(score(query, high[...]) if i == blocks - 1 else near_ref[i, 2])
        scores.extend([exp_ref[i, near], exp_ref[i, near + 1]])
        last = score(query, block_rows(whole, lists_ref[i, LISTED + 2]))
        scores.append(present(last, lists_ref[i, near + 2]))
        peak = scores[0]
        for part in scores[1:]:
            peak = jnp.maximum(peak, part)
        peak = jnp.max(peak, axis=1, keepdims=True)
        exps = [jnp.exp(part - peak) for part in scores]
        for slot, value in enumerate(exps):
            exp_ref[i, slot] = value
        scale = 1.0 / row_total(exps)
        add_columns(sums_ref, lists_ref, i, [value * scale for value in exps])
    sent_ref[...] = sums_ref[...].astype(sent_ref.dtype)


def scaled(exp_ref, lists_ref, i, factor_refs):
    parts = []
    for slot in range(exp_ref.shape[1]):
        value = exp_ref[i, slot]
        for factor in factor_refs:
            value = value * factor[pl.ds(jnp.maximum(lists_ref[i, slot], 0), 1), :]
        parts.append(value)
    return parts


def round_kernel(
    blocks, lists_hbm, exp_ref, sum_a, sum_b, factor_ref, sums_ref, sent_ref, lists_ref, sem
):
    load(lists_hbm, lists_ref, sem)
    factor_ref[...] = 1.0 / (sum_a[...] + sum_b[...].astype(jnp.float32))
    sums_ref[...] = jnp.zeros_like(sums_ref)
    for i in range(blocks):
        parts = scaled(exp_ref, lists_ref, i, [factor_ref])
        scale = 1.0 / row_total(parts)
        add_columns(sums_ref, lists_ref, i, [part * scale for part in parts])
    sent_ref[...] = sums_ref[...].astype(sent_ref.dtype)


def output_kernel(
    blocks, caps, lists_hbm, exp_ref, factor_ref, sum_a, sum_b, own, low, high,
    near_far, other_far, wide, slim, rest, out_ref, last_ref, whole, partial_ref, weight_ref,
    lists_ref, sems,
):
    gathered = Whole(caps, wide, slim, rest, whole, lists_hbm, lists_ref, sems)
    gathered.start()
    last_ref[...] = 1.0 / (sum_a[...] + sum_b[...].astype(jnp.float32))
    gathered.lists.wait()
    for i in range(blocks):
        parts = scaled(exp_ref, lists_ref, i, [factor_ref, last_ref])
        scale = 1.0 / row_total(parts)
        values = near_blocks(i, blocks, own, low, high)
        values += far_blocks(i, lists_ref, (near_far, other_far))
        parts = [(part * scale).astype(jnp.bfloat16) for part in parts]
        total = None
        for part, value in zip(parts, values):
            term = jnp.dot(part, value, preferred_element_type=jnp.float32)
            total = term if total is None else total + term
        partial_ref[i] = total
        weight_ref[i] = parts[-1]
    gathered.wait()
    for i in range(blocks):
        value = block_rows(whole, lists_ref[i, LISTED + 2])
        total = partial_ref[i] + jnp.dot(weight_ref[i], value, preferred_element_type=jnp.float32)
        out_ref[pl.ds(i * BLOCK, BLOCK), :] = total.astype(out_ref.dtype)


def shifted(x, axis, by):
    devices = lax.axis_size(axis)
    return lax.ppermute(x, axis, [(i, (i + by) % devices) for i in range(devices)])


def swapped(x):
    return lax.ppermute(x, "rep", [(0, 1), (1, 0)])


def over_seq(mine, sent):
    devices = lax.axis_size("seq")
    pairs = lambda by: [(i, i ^ by) for i in range(devices)]
    if devices <= 4:
        parts = [lax.ppermute(sent, "seq", pairs(by)) for by in reversed(range(1, devices))]
        return sum([part.astype(mine.dtype) for part in parts], mine)
    by = 1
    while by < devices:
        mine = mine + lax.ppermute(mine, "seq", pairs(by))
        by *= 2
    return mine


def two_away(wide, slim):
    chips = lax.axis_size("seq")
    moves = [(i, (i - 2) % chips) for i in range(chips)]
    axes = ("seq", "rep")
    return (
        lax.ppermute(wide, axes, [(2 * i, 2 * j) for i, j in moves]),
        lax.ppermute(slim, axes, [(2 * i + 1, 2 * j + 1) for i, j in moves]),
    )


def remainder(crowded, *rest):
    return lax.cond(
        crowded,
        lambda *x: tuple(shifted(part, "seq", -2) for part in x),
        lambda *x: x,
        *rest,
    )


def with_swap(near, wide, rest, caps, rep):
    beyond = jnp.concatenate([wide, rest[(caps[0] - caps[1]) * BLOCK :]], axis=0)
    return swapped(jnp.where(rep == 0, beyond, near))


def body(queries, key_rows, value_rows, pattern):
    tok_local, heads_local, width = queries.shape
    assert heads_local == 1
    blocks = tok_local // BLOCK
    list_len = pattern.shape[1]
    far_count = list_len - 3
    total_blocks = pattern.shape[0]
    axes = ("seq", "rep")
    shards = lax.axis_size(axes)
    rep = lax.axis_index("rep")
    q = queries.reshape(tok_local, width)
    k = key_rows.reshape(tok_local, width)
    v = value_rows.reshape(tok_local, width)

    caps = (blocks - blocks // 8, blocks - blocks // 2)
    columns = pattern.T
    k_near = shifted(k, "seq", -1)
    k_wide, k_slim, k_rest = pack_keys(blocks, shards, caps, columns, k)
    k_in, columns, k_wide, k_slim, k_rest = lax.optimization_barrier(
        (k, columns, k_wide, k_slim, k_rest)
    )
    *v_packs, edges_low, edges_high, near_scores, q_held, lists, crowded = plan(
        blocks, shards, caps, columns, q, k_in, v
    )
    v_wide, v_slim, v_rest = v_packs
    k_wide, k_slim = two_away(k_wide, k_slim)
    k_rest, v_rest = remainder(crowded[0] > 0, k_rest, v_rest)
    low = shifted(edges_low, axes, 1)
    high = shifted(edges_high, axes, -1)

    near_scores, v_in = lax.optimization_barrier((near_scores, v))
    v_near = shifted(v_in, "seq", -1)
    k_near, k_wide, k_slim = lax.optimization_barrier((k_near, k_wide, k_slim))
    k_other = with_swap(k_near, k_wide, k_rest, caps, rep)
    exps, sums, sent = pl.pallas_call(
        lambda *refs: score_kernel(blocks, caps, *refs),
        out_shape=(
            jax.ShapeDtypeStruct((blocks, list_len, BLOCK, BLOCK), jnp.float32),
            jax.ShapeDtypeStruct((total_blocks, BLOCK), jnp.float32),
            jax.ShapeDtypeStruct((total_blocks, BLOCK), SENT),
        ),
        in_specs=[HBM] + [VMEM] * 8 + [ANY],
        out_specs=(VMEM, VMEM, VMEM),
        scratch_shapes=[
            pltpu.VMEM((tok_local, width), jnp.bfloat16),
            pltpu.SMEM((blocks, 2 * list_len - 3), jnp.int32),
            pltpu.SemaphoreType.DMA((2,)),
        ],
        cost_estimate=pl.CostEstimate(flops=100663296, bytes_accessed=6291456, transcendentals=786432),
        compiler_params=pltpu.CompilerParams(vmem_limit_bytes=LIMIT),
    )(
        lists, q_held, near_scores, low[:, :width], high[:, :width],
        k_near, k_other, k_wide, k_slim, k_rest,
    )

    v_wide, v_slim, sent = lax.optimization_barrier((v_wide, v_slim, sent))
    mine = over_seq(sums, sent)
    v_wide, v_slim = two_away(v_wide, v_slim)
    mine, v_near = lax.optimization_barrier((mine, v_near))
    v_wide, v_slim = lax.optimization_barrier((v_wide, v_slim))
    factor, sums, sent = pl.pallas_call(
        lambda *refs: round_kernel(blocks, *refs),
        out_shape=(
            jax.ShapeDtypeStruct((total_blocks, BLOCK), jnp.float32),
            jax.ShapeDtypeStruct((total_blocks, BLOCK), jnp.float32),
            jax.ShapeDtypeStruct((total_blocks, BLOCK), SENT),
        ),
        in_specs=[HBM] + [VMEM] * 3,
        out_specs=(VMEM, VMEM, VMEM),
        scratch_shapes=[
            pltpu.SMEM((blocks, 2 * list_len - 3), jnp.int32),
            pltpu.SemaphoreType.DMA,
        ],
        cost_estimate=pl.CostEstimate(flops=7864320, bytes_accessed=4194304, transcendentals=0),
        compiler_params=pltpu.CompilerParams(vmem_limit_bytes=LIMIT),
    )(lists, exps, mine, swapped(mine))

    v_far, factor = lax.optimization_barrier(((v_near, v_wide, v_rest), factor))
    v_near, v_wide, v_rest = v_far
    v_other = with_swap(v_near, v_wide, v_rest, caps, rep)
    mine = over_seq(sums, sent)
    out = pl.pallas_call(
        lambda *refs: output_kernel(blocks, caps, *refs),
        out_shape=jax.ShapeDtypeStruct((tok_local, width), jnp.bfloat16),
        in_specs=[HBM] + [VMEM] * 11 + [ANY],
        out_specs=VMEM,
        scratch_shapes=[
            pltpu.VMEM((total_blocks, BLOCK), jnp.float32),
            pltpu.VMEM((tok_local, width), jnp.bfloat16),
            pltpu.VMEM((blocks, BLOCK, width), jnp.float32),
            pltpu.VMEM((blocks, BLOCK, BLOCK), jnp.bfloat16),
            pltpu.SMEM((blocks, 2 * list_len - 3), jnp.int32),
            pltpu.SemaphoreType.DMA((2,)),
        ],
        cost_estimate=pl.CostEstimate(flops=201326592, bytes_accessed=6291456, transcendentals=0),
        compiler_params=pltpu.CompilerParams(vmem_limit_bytes=LIMIT),
    )(
        lists, exps, factor, mine, swapped(mine), v, low[:, width:], high[:, width:],
        v_near, v_other, v_wide, v_slim, v_rest,
    )
    return out.reshape(tok_local, heads_local, width)


def solution(mesh):
    in_specs = (
        P(("groups", "seq", "rep"), "head", None),
        P(("groups", "seq", "rep"), "head", None),
        P(("groups", "seq", "rep"), "head", None),
        P("groups", None),
    )
    out_specs = P(("groups", "seq", "rep"), "head", None)
    return jax.shard_map(body, mesh=mesh, in_specs=in_specs, out_specs=out_specs, check_vma=False)
```

```python
import math

import jax
import jax.numpy as jnp
from jax import lax
from jax.experimental import pallas as pl
from jax.experimental.pallas import tpu as pltpu
from jax.sharding import PartitionSpec as P

BLOCK = 128
ITERS = 2
LISTED = 6
SENT = jnp.bfloat16
VMEM = pl.BlockSpec(memory_space=pltpu.VMEM)
ANY = pl.BlockSpec(memory_space=pl.ANY)
HBM = pl.BlockSpec(memory_space=pltpu.HBM)
SMEM = pl.BlockSpec(memory_space=pltpu.SMEM)
LIMIT = 32 * 1024 * 1024


def block_rows(ref, index):
    start = index * BLOCK
    if not isinstance(index, int):
        start = pl.multiple_of(start, BLOCK)
    return ref[pl.ds(start, BLOCK), :]


def near_blocks(i, blocks, own, low, high):
    before = low[...] if i == 0 else block_rows(own, i - 1)
    after = high[...] if i == blocks - 1 else block_rows(own, i + 1)
    return [block_rows(own, i), before, after]


def far_blocks(i, lists_ref, fars):
    return [block_rows(far, lists_ref[i, LISTED + slot]) for slot, far in enumerate(fars)]


def score(query, key):
    product = lax.dot_general(
        query, key, (((1,), (1,)), ((), ())), preferred_element_type=jnp.float32
    )
    return product * (1.0 / math.sqrt(key.shape[1]))


def add_columns(sums_ref, lists_ref, i, weights):
    for slot, weight in enumerate(weights):
        at = pl.ds(jnp.maximum(lists_ref[i, slot], 0), 1)
        sums_ref[at, :] += jnp.sum(weight, axis=0, keepdims=True)


def row_total(parts):
    total = parts[0]
    for part in parts[1:]:
        total = total + part
    return jnp.sum(total, axis=1, keepdims=True)


def listed_bits(pattern_ref, blocks, shards, source, first_core):
    wanted = jnp.int32(0)
    for back, column, counted in ((4, 5, True), (3, 4, first_core)):
        if counted is False:
            continue
        first = (source + shards - back) % shards * blocks
        for i in range(blocks):
            entry = pattern_ref[column, first + i]
            bit = jnp.left_shift(jnp.int32(1), jnp.maximum(entry - source * blocks, 0))
            hit = entry >= 0 if counted is True else (entry >= 0) & counted
            wanted = jnp.where(hit, wanted | bit, wanted)
    return [jnp.bitwise_and(jnp.right_shift(wanted, b), 1) for b in range(blocks)]


class Copies:
    def __init__(self, sems):
        self.sems, self.started = sems, []

    def start(self, source, target):
        copy = pltpu.make_async_copy(source, target, self.sems.at[len(self.started)])
        copy.start()
        self.started.append(copy)

    def wait(self):
        for copy in self.started:
            copy.wait()


def pack(pattern_ref, blocks, shards, caps, rows, outs, order_ref, copies):
    position, rep = lax.axis_index(("seq", "rep")), lax.axis_index("rep")
    bits = listed_bits(pattern_ref, blocks, shards, position, rep == 0)
    rank, spare = jnp.int32(0), sum(bits)
    for b, bit in enumerate(bits):
        order_ref[jnp.where(bit == 1, rank, spare)] = b
        rank, spare = rank + bit, spare + 1 - bit
    for out, first in zip(outs, (0, 0, caps[1])):
        for t in range(out.shape[0] // BLOCK):
            begin = pl.multiple_of(order_ref[first + t] * BLOCK, BLOCK)
            copies.start(rows.at[pl.ds(begin, BLOCK), :], out.at[pl.ds(t * BLOCK, BLOCK), :])


def load(source, target, sem):
    copy = pltpu.make_async_copy(source, target, sem)
    copy.start()
    copy.wait()


def key_kernel(blocks, shards, caps, pattern_hbm, k_ref, *refs):
    outs, (pattern_ref, order_ref, sems, sem) = refs[:3], refs[3:]
    load(pattern_hbm, pattern_ref, sem)
    copies = Copies(sems)
    pack(pattern_ref, blocks, shards, caps, k_ref, outs, order_ref, copies)
    copies.wait()


def plan_kernel(blocks, shards, caps, pattern_hbm, q_hbm, k_ref, v_ref, *refs):
    outs, edges = refs[:3], refs[3:5]
    score_ref, q_ref, lists_ref, crowded_ref = refs[5:9]
    own, pattern_ref, order_ref, rank_ref, sems, near_sems, sem = refs[9:]
    position, rep = lax.axis_index(("seq", "rep")), lax.axis_index("rep")
    width = k_ref.shape[1]
    held = Copies(near_sems)
    held.start(q_hbm, q_ref)
    held.start(k_ref, own)
    copies = Copies(sems)
    for edge, begin in zip(edges, ((blocks - 1) * BLOCK, 0)):
        for at, rows in enumerate((k_ref, v_ref)):
            copies.start(rows.at[pl.ds(begin, BLOCK), :], edge.at[:, pl.ds(at * width, width)])
    load(pattern_hbm, pattern_ref, sem)
    pack(pattern_ref, blocks, shards, caps, v_ref, outs, order_ref, copies)
    for at, ahead in enumerate((3, 4)):
        source = lax.rem(position + ahead, shards)
        bits = listed_bits(
            pattern_ref, blocks, shards, source, (rep == 0) if ahead == 4 else True
        )
        rank = jnp.int32(0)
        for b, bit in enumerate(bits):
            rank_ref[at, b] = rank if ahead == 4 else jnp.where(rep == 1, rank, b)
            rank = rank + bit
    for i in range(blocks):
        for slot in range(pattern_ref.shape[0]):
            entry = pattern_ref[slot, position * blocks + i]
            lists_ref[i, slot] = entry
            if slot >= 3:
                source = lax.rem(position + slot - 1, shards)
                at = jnp.where(entry >= 0, entry - source * blocks, 0)
                at = at if slot == 3 else rank_ref[slot - 4, at]
                lists_ref[i, pattern_ref.shape[0] + slot - 3] = at
    crowded = jnp.int32(0)
    for source in range(shards):
        count = sum(listed_bits(pattern_ref, blocks, shards, source, source % 2 == 0))
        crowded = jnp.maximum(crowded, jnp.where(count > caps[source % 2], 1, 0))
    crowded_ref[0] = crowded
    held.wait()
    for i in range(blocks):
        query = block_rows(q_ref, i)
        for slot, other in enumerate((i, i - 1, i + 1)):
            if 0 <= other < blocks:
                score_ref[i, slot] = score(query, block_rows(own, other))
    copies.wait()


def packed_shapes(blocks, caps, rows):
    sizes = (caps[0], caps[1], blocks - caps[1])
    return [jax.ShapeDtypeStruct((n * BLOCK, rows.shape[1]), rows.dtype) for n in sizes]


def pack_keys(blocks, shards, caps, columns, k):
    return pl.pallas_call(
        lambda *refs: key_kernel(blocks, shards, caps, *refs),
        out_shape=packed_shapes(blocks, caps, k),
        in_specs=[HBM] * 2,
        out_specs=[VMEM] * 3,
        scratch_shapes=[
            pltpu.SMEM(columns.shape, jnp.int32),
            pltpu.SMEM((blocks,), jnp.int32),
            pltpu.SemaphoreType.DMA((2 * blocks,)),
            pltpu.SemaphoreType.DMA,
        ],
    )(columns, k)


def plan(blocks, shards, caps, columns, q, k, v):
    width, list_len = k.shape[1], columns.shape[0]
    return pl.pallas_call(
        lambda *refs: plan_kernel(blocks, shards, caps, *refs),
        out_shape=packed_shapes(blocks, caps, v)
        + [jax.ShapeDtypeStruct((BLOCK, 2 * width), k.dtype)] * 2
        + [
            jax.ShapeDtypeStruct((blocks, 3, BLOCK, BLOCK), jnp.float32),
            jax.ShapeDtypeStruct(q.shape, q.dtype),
            jax.ShapeDtypeStruct((blocks, 2 * list_len - 3), jnp.int32),
            jax.ShapeDtypeStruct((1,), jnp.int32),
        ],
        in_specs=[HBM] * 4,
        out_specs=[VMEM] * 7 + [SMEM] * 2,
        scratch_shapes=[
            pltpu.VMEM(k.shape, k.dtype),
            pltpu.SMEM(columns.shape, jnp.int32),
            pltpu.SMEM((blocks,), jnp.int32),
            pltpu.SMEM((2, blocks), jnp.int32),
            pltpu.SemaphoreType.DMA((2 * blocks + 4,)),
            pltpu.SemaphoreType.DMA((2,)),
            pltpu.SemaphoreType.DMA,
        ],
        cost_estimate=pl.CostEstimate(flops=100663296, bytes_accessed=4194304, transcendentals=0),
        compiler_params=pltpu.CompilerParams(vmem_limit_bytes=LIMIT),
    )(columns, q, k, v)


class Whole:
    def __init__(self, caps, wide, slim, rest, whole, lists_hbm, lists_ref, sems):
        self.parts = (0, wide, caps[0] - caps[1]), (1, slim, 0)
        self.rest, self.whole, self.sem = rest, whole, sems.at[0]
        self.lists = pltpu.make_async_copy(lists_hbm, lists_ref, sems.at[1])

    def left(self, used, skip):
        count = self.whole.shape[0] - used
        return pltpu.make_async_copy(
            self.rest.at[pl.ds(skip * BLOCK, count), :], self.whole.at[pl.ds(used, count), :], self.sem
        )

    def on_core(self, act):
        for core, first, skip in self.parts:

            @pl.when(lax.axis_index("rep") == core)
            def _():
                act(first, skip)

    def start(self):
        self.lists.start()

        def begin(first, skip):
            self.left(first.shape[0], skip).start()
            self.whole[: first.shape[0], :] = first[...]

        self.on_core(begin)

    def wait(self):
        self.on_core(lambda first, skip: self.left(first.shape[0], skip).wait())


def present(scores, entry):
    return scores + jnp.where(entry >= 0, 0.0, -jnp.inf).astype(jnp.float32)


def score_kernel(
    blocks, caps, lists_hbm, q_ref, near_ref, low, high,
    near_far, other_far, wide, slim, rest, exp_ref, sums_ref, sent_ref,
    whole, lists_ref, sems,
):
    gathered = Whole(caps, wide, slim, rest, whole, lists_hbm, lists_ref, sems)
    gathered.start()
    near = near_ref.shape[1]
    sums_ref[...] = jnp.zeros_like(sums_ref)
    gathered.lists.wait()
    for i in range(blocks):
        query = block_rows(q_ref, i)
        for slot, key in enumerate(far_blocks(i, lists_ref, (near_far, other_far))):
            exp_ref[i, near + slot] = present(score(query, key), lists_ref[i, near + slot])
    gathered.wait()
    for i in range(blocks):
        query = block_rows(q_ref, i)
        scores = [near_ref[i, 0]]
        scores.append(score(query, low[...]) if i == 0 else near_ref[i, 1])
        scores.append(score(query, high[...]) if i == blocks - 1 else near_ref[i, 2])
        scores.extend([exp_ref[i, near], exp_ref[i, near + 1]])
        last = score(query, block_rows(whole, lists_ref[i, LISTED + 2]))
        scores.append(present(last, lists_ref[i, near + 2]))
        peak = scores[0]
        for part in scores[1:]:
            peak = jnp.maximum(peak, part)
        peak = jnp.max(peak, axis=1, keepdims=True)
        exps = [jnp.exp(part - peak) for part in scores]
        for slot, value in enumerate(exps):
            exp_ref[i, slot] = value
        scale = 1.0 / row_total(exps)
        add_columns(sums_ref, lists_ref, i, [value * scale for value in exps])
    sent_ref[...] = sums_ref[...].astype(sent_ref.dtype)


def scaled(exp_ref, lists_ref, i, factor_refs):
    parts = []
    for slot in range(exp_ref.shape[1]):
        value = exp_ref[i, slot]
        for factor in factor_refs:
            value = value * factor[pl.ds(jnp.maximum(lists_ref[i, slot], 0), 1), :]
        parts.append(value)
    return parts


def round_kernel(
    blocks, lists_hbm, exp_ref, sum_a, sum_b, factor_ref, sums_ref, sent_ref, lists_ref, sem
):
    load(lists_hbm, lists_ref, sem)
    factor_ref[...] = 1.0 / (sum_a[...] + sum_b[...].astype(jnp.float32))
    sums_ref[...] = jnp.zeros_like(sums_ref)
    for i in range(blocks):
        parts = scaled(exp_ref, lists_ref, i, [factor_ref])
        scale = 1.0 / row_total(parts)
        add_columns(sums_ref, lists_ref, i, [part * scale for part in parts])
    sent_ref[...] = sums_ref[...].astype(sent_ref.dtype)


def output_kernel(
    blocks, caps, lists_hbm, exp_ref, factor_ref, sum_a, sum_b, own, low, high,
    near_far, other_far, wide, slim, rest, out_ref, last_ref, whole,
    lists_ref, sems,
):
    gathered = Whole(caps, wide, slim, rest, whole, lists_hbm, lists_ref, sems)
    gathered.start()
    last_ref[...] = 1.0 / (sum_a[...] + sum_b[...].astype(jnp.float32))
    gathered.lists.wait()
    gathered.wait()
    for i in range(blocks):
        parts = scaled(exp_ref, lists_ref, i, [factor_ref, last_ref])
        scale = 1.0 / row_total(parts)
        values = near_blocks(i, blocks, own, low, high)
        values += far_blocks(i, lists_ref, (near_far, other_far, whole))
        total = None
        for part, value in zip(parts, values):
            part = (part * scale).astype(jnp.bfloat16)
            term = jnp.dot(part, value, preferred_element_type=jnp.float32)
            total = term if total is None else total + term
        out_ref[pl.ds(i * BLOCK, BLOCK), :] = total.astype(out_ref.dtype)


def shifted(x, axis, by):
    devices = lax.axis_size(axis)
    return lax.ppermute(x, axis, [(i, (i + by) % devices) for i in range(devices)])


def swapped(x):
    return lax.ppermute(x, "rep", [(0, 1), (1, 0)])


def over_seq(mine, sent):
    devices = lax.axis_size("seq")
    pairs = lambda by: [(i, i ^ by) for i in range(devices)]
    if devices <= 4:
        parts = [lax.ppermute(sent, "seq", pairs(by)) for by in reversed(range(1, devices))]
        return sum([part.astype(mine.dtype) for part in parts], mine)
    by = 1
    while by < devices:
        mine = mine + lax.ppermute(mine, "seq", pairs(by))
        by *= 2
    return mine


def two_away(wide, slim):
    chips = lax.axis_size("seq")
    moves = [(i, (i - 2) % chips) for i in range(chips)]
    axes = ("seq", "rep")
    return (
        lax.ppermute(wide, axes, [(2 * i, 2 * j) for i, j in moves]),
        lax.ppermute(slim, axes, [(2 * i + 1, 2 * j + 1) for i, j in moves]),
    )


def remainder(crowded, *rest):
    return lax.cond(
        crowded,
        lambda *x: tuple(shifted(part, "seq", -2) for part in x),
        lambda *x: x,
        *rest,
    )


def with_swap(near, wide, rest, caps, rep):
    beyond = jnp.concatenate([wide, rest[(caps[0] - caps[1]) * BLOCK :]], axis=0)
    return swapped(jnp.where(rep == 0, beyond, near))


def body(queries, key_rows, value_rows, pattern):
    tok_local, heads_local, width = queries.shape
    assert heads_local == 1
    blocks = tok_local // BLOCK
    list_len = pattern.shape[1]
    far_count = list_len - 3
    total_blocks = pattern.shape[0]
    axes = ("seq", "rep")
    shards = lax.axis_size(axes)
    rep = lax.axis_index("rep")
    q = queries.reshape(tok_local, width)
    k = key_rows.reshape(tok_local, width)
    v = value_rows.reshape(tok_local, width)

    caps = (blocks - blocks // 8, blocks - blocks // 2)
    columns = pattern.T
    k_near = shifted(k, "seq", -1)
    k_wide, k_slim, k_rest = pack_keys(blocks, shards, caps, columns, k)
    k_in, columns, k_wide, k_slim, k_rest = lax.optimization_barrier(
        (k, columns, k_wide, k_slim, k_rest)
    )
    *v_packs, edges_low, edges_high, near_scores, q_held, lists, crowded = plan(
        blocks, shards, caps, columns, q, k_in, v
    )
    v_wide, v_slim, v_rest = v_packs
    k_wide, k_slim = two_away(k_wide, k_slim)
    k_rest, v_rest = remainder(crowded[0] > 0, k_rest, v_rest)
    low = shifted(edges_low, axes, 1)
    high = shifted(edges_high, axes, -1)

    near_scores, v_in = lax.optimization_barrier((near_scores, v))
    v_near = shifted(v_in, "seq", -1)
    k_near, k_wide, k_slim = lax.optimization_barrier((k_near, k_wide, k_slim))
    k_other = with_swap(k_near, k_wide, k_rest, caps, rep)
    exps, sums, sent = pl.pallas_call(
        lambda *refs: score_kernel(blocks, caps, *refs),
        out_shape=(
            jax.ShapeDtypeStruct((blocks, list_len, BLOCK, BLOCK), jnp.float32),
            jax.ShapeDtypeStruct((total_blocks, BLOCK), jnp.float32),
            jax.ShapeDtypeStruct((total_blocks, BLOCK), SENT),
        ),
        in_specs=[HBM] + [VMEM] * 8 + [ANY],
        out_specs=(VMEM, VMEM, VMEM),
        scratch_shapes=[
            pltpu.VMEM((tok_local, width), jnp.bfloat16),
            pltpu.SMEM((blocks, 2 * list_len - 3), jnp.int32),
            pltpu.SemaphoreType.DMA((2,)),
        ],
        cost_estimate=pl.CostEstimate(flops=100663296, bytes_accessed=6291456, transcendentals=786432),
        compiler_params=pltpu.CompilerParams(vmem_limit_bytes=LIMIT),
    )(
        lists, q_held, near_scores, low[:, :width], high[:, :width],
        k_near, k_other, k_wide, k_slim, k_rest,
    )

    v_wide, v_slim, sent = lax.optimization_barrier((v_wide, v_slim, sent))
    mine = over_seq(sums, sent)
    v_wide, v_slim = two_away(v_wide, v_slim)
    mine, v_near = lax.optimization_barrier((mine, v_near))
    v_wide, v_slim = lax.optimization_barrier((v_wide, v_slim))
    factor, sums, sent = pl.pallas_call(
        lambda *refs: round_kernel(blocks, *refs),
        out_shape=(
            jax.ShapeDtypeStruct((total_blocks, BLOCK), jnp.float32),
            jax.ShapeDtypeStruct((total_blocks, BLOCK), jnp.float32),
            jax.ShapeDtypeStruct((total_blocks, BLOCK), SENT),
        ),
        in_specs=[HBM] + [VMEM] * 3,
        out_specs=(VMEM, VMEM, VMEM),
        scratch_shapes=[
            pltpu.SMEM((blocks, 2 * list_len - 3), jnp.int32),
            pltpu.SemaphoreType.DMA,
        ],
        cost_estimate=pl.CostEstimate(flops=7864320, bytes_accessed=4194304, transcendentals=0),
        compiler_params=pltpu.CompilerParams(vmem_limit_bytes=LIMIT),
    )(lists, exps, mine, swapped(mine))

    v_far, factor = lax.optimization_barrier(((v_near, v_wide, v_rest), factor))
    v_near, v_wide, v_rest = v_far
    v_other = with_swap(v_near, v_wide, v_rest, caps, rep)
    mine = over_seq(sums, sent)
    out = pl.pallas_call(
        lambda *refs: output_kernel(blocks, caps, *refs),
        out_shape=jax.ShapeDtypeStruct((tok_local, width), jnp.bfloat16),
        in_specs=[HBM] + [VMEM] * 11 + [ANY],
        out_specs=VMEM,
        scratch_shapes=[
            pltpu.VMEM((total_blocks, BLOCK), jnp.float32),
            pltpu.VMEM((tok_local, width), jnp.bfloat16),
            pltpu.SMEM((blocks, 2 * list_len - 3), jnp.int32),
            pltpu.SemaphoreType.DMA((2,)),
        ],
        cost_estimate=pl.CostEstimate(flops=201326592, bytes_accessed=6291456, transcendentals=0),
        compiler_params=pltpu.CompilerParams(vmem_limit_bytes=LIMIT),
    )(
        lists, exps, factor, mine, swapped(mine), v, low[:, width:], high[:, width:],
        v_near, v_other, v_wide, v_slim, v_rest,
    )
    return out.reshape(tok_local, heads_local, width)


def solution(mesh):
    in_specs = (
        P(("groups", "seq", "rep"), "head", None),
        P(("groups", "seq", "rep"), "head", None),
        P(("groups", "seq", "rep"), "head", None),
        P("groups", None),
    )
    out_specs = P(("groups", "seq", "rep"), "head", None)
    return jax.shard_map(body, mesh=mesh, in_specs=in_specs, out_specs=out_specs, check_vma=False)
```

```python
import math

import jax
import jax.numpy as jnp
from jax import lax
from jax.experimental import pallas as pl
from jax.experimental.pallas import tpu as pltpu
from jax.sharding import PartitionSpec as P

BLOCK = 128
ITERS = 2
LISTED = 6
SENT = jnp.bfloat16
VMEM = pl.BlockSpec(memory_space=pltpu.VMEM)
ANY = pl.BlockSpec(memory_space=pl.ANY)
HBM = pl.BlockSpec(memory_space=pltpu.HBM)
SMEM = pl.BlockSpec(memory_space=pltpu.SMEM)
LIMIT = 32 * 1024 * 1024


def block_rows(ref, index):
    start = index * BLOCK
    if not isinstance(index, int):
        start = pl.multiple_of(start, BLOCK)
    return ref[pl.ds(start, BLOCK), :]


def near_blocks(i, blocks, own, low, high):
    before = low[...] if i == 0 else block_rows(own, i - 1)
    after = high[...] if i == blocks - 1 else block_rows(own, i + 1)
    return [block_rows(own, i), before, after]


def far_blocks(i, lists_ref, fars):
    return [block_rows(far, lists_ref[i, LISTED + slot]) for slot, far in enumerate(fars)]


def score(query, key):
    product = lax.dot_general(
        query, key, (((1,), (1,)), ((), ())), preferred_element_type=jnp.float32
    )
    return product * (1.0 / math.sqrt(key.shape[1]))


def add_columns(sums_ref, lists_ref, i, weights):
    for slot, weight in enumerate(weights):
        at = pl.ds(jnp.maximum(lists_ref[i, slot], 0), 1)
        sums_ref[at, :] += jnp.sum(weight, axis=0, keepdims=True)


def row_total(parts):
    total = parts[0]
    for part in parts[1:]:
        total = total + part
    return jnp.sum(total, axis=1, keepdims=True)


def listed_bits(pattern_ref, blocks, shards, source, first_core):
    wanted = jnp.int32(0)
    for back, column, counted in ((4, 5, True), (3, 4, first_core)):
        if counted is False:
            continue
        first = (source + shards - back) % shards * blocks
        for i in range(blocks):
            entry = pattern_ref[column, first + i]
            bit = jnp.left_shift(jnp.int32(1), jnp.maximum(entry - source * blocks, 0))
            hit = entry >= 0 if counted is True else (entry >= 0) & counted
            wanted = jnp.where(hit, wanted | bit, wanted)
    return [jnp.bitwise_and(jnp.right_shift(wanted, b), 1) for b in range(blocks)]


class Copies:
    def __init__(self, sems):
        self.sems, self.started = sems, []

    def start(self, source, target):
        copy = pltpu.make_async_copy(source, target, self.sems.at[len(self.started)])
        copy.start()
        self.started.append(copy)

    def wait(self):
        for copy in self.started:
            copy.wait()


def pack(pattern_ref, blocks, shards, caps, rows, outs, order_ref, copies):
    position, rep = lax.axis_index(("seq", "rep")), lax.axis_index("rep")
    bits = listed_bits(pattern_ref, blocks, shards, position, rep == 0)
    rank, spare = jnp.int32(0), sum(bits)
    for b, bit in enumerate(bits):
        order_ref[jnp.where(bit == 1, rank, spare)] = b
        rank, spare = rank + bit, spare + 1 - bit
    for out, first in zip(outs, (0, 0, caps[1])):
        for t in range(out.shape[0] // BLOCK):
            begin = pl.multiple_of(order_ref[first + t] * BLOCK, BLOCK)
            copies.start(rows.at[pl.ds(begin, BLOCK), :], out.at[pl.ds(t * BLOCK, BLOCK), :])


def load(source, target, sem):
    copy = pltpu.make_async_copy(source, target, sem)
    copy.start()
    copy.wait()


def key_kernel(blocks, shards, caps, pattern_hbm, k_ref, *refs):
    outs, (pattern_ref, order_ref, sems, sem) = refs[:3], refs[3:]
    load(pattern_hbm, pattern_ref, sem)
    copies = Copies(sems)
    pack(pattern_ref, blocks, shards, caps, k_ref, outs, order_ref, copies)
    copies.wait()


def plan_kernel(blocks, shards, caps, pattern_hbm, q_hbm, k_ref, v_ref, *refs):
    outs, edges = refs[:3], refs[3:5]
    score_ref, q_ref, lists_ref, crowded_ref = refs[5:9]
    own, pattern_ref, order_ref, rank_ref, sems, near_sems, sem = refs[9:]
    position, rep = lax.axis_index(("seq", "rep")), lax.axis_index("rep")
    width = k_ref.shape[1]
    held = Copies(near_sems)
    held.start(q_hbm, q_ref)
    held.start(k_ref, own)
    copies = Copies(sems)
    for edge, begin in zip(edges, ((blocks - 1) * BLOCK, 0)):
        for at, rows in enumerate((k_ref, v_ref)):
            copies.start(rows.at[pl.ds(begin, BLOCK), :], edge.at[:, pl.ds(at * width, width)])
    load(pattern_hbm, pattern_ref, sem)
    pack(pattern_ref, blocks, shards, caps, v_ref, outs, order_ref, copies)
    for at, ahead in enumerate((3, 4)):
        source = lax.rem(position + ahead, shards)
        bits = listed_bits(
            pattern_ref, blocks, shards, source, (rep == 0) if ahead == 4 else True
        )
        rank = jnp.int32(0)
        for b, bit in enumerate(bits):
            rank_ref[at, b] = rank if ahead == 4 else jnp.where(rep == 1, rank, b)
            rank = rank + bit
    for i in range(blocks):
        for slot in range(pattern_ref.shape[0]):
            entry = pattern_ref[slot, position * blocks + i]
            lists_ref[i, slot] = entry
            if slot >= 3:
                source = lax.rem(position + slot - 1, shards)
                at = jnp.where(entry >= 0, entry - source * blocks, 0)
                at = at if slot == 3 else rank_ref[slot - 4, at]
                lists_ref[i, pattern_ref.shape[0] + slot - 3] = at
    crowded = jnp.int32(0)
    for source in range(shards):
        count = sum(listed_bits(pattern_ref, blocks, shards, source, source % 2 == 0))
        crowded = jnp.maximum(crowded, jnp.where(count > caps[source % 2], 1, 0))
    crowded_ref[0] = crowded
    held.wait()
    for i in range(blocks):
        query = block_rows(q_ref, i)
        for slot, other in enumerate((i, i - 1, i + 1)):
            if 0 <= other < blocks:
                score_ref[i, slot] = score(query, block_rows(own, other))
    copies.wait()


def packed_shapes(blocks, caps, rows):
    sizes = (caps[0], caps[1], blocks - caps[1])
    return [jax.ShapeDtypeStruct((n * BLOCK, rows.shape[1]), rows.dtype) for n in sizes]


def pack_keys(blocks, shards, caps, columns, k):
    return pl.pallas_call(
        lambda *refs: key_kernel(blocks, shards, caps, *refs),
        out_shape=packed_shapes(blocks, caps, k),
        in_specs=[HBM] * 2,
        out_specs=[VMEM] * 3,
        scratch_shapes=[
            pltpu.SMEM(columns.shape, jnp.int32),
            pltpu.SMEM((blocks,), jnp.int32),
            pltpu.SemaphoreType.DMA((2 * blocks,)),
            pltpu.SemaphoreType.DMA,
        ],
    )(columns, k)


def plan(blocks, shards, caps, columns, q, k, v):
    width, list_len = k.shape[1], columns.shape[0]
    return pl.pallas_call(
        lambda *refs: plan_kernel(blocks, shards, caps, *refs),
        out_shape=packed_shapes(blocks, caps, v)
        + [jax.ShapeDtypeStruct((BLOCK, 2 * width), k.dtype)] * 2
        + [
            jax.ShapeDtypeStruct((blocks, 3, BLOCK, BLOCK), jnp.float32),
            jax.ShapeDtypeStruct(q.shape, q.dtype),
            jax.ShapeDtypeStruct((blocks, 2 * list_len - 3), jnp.int32),
            jax.ShapeDtypeStruct((1,), jnp.int32),
        ],
        in_specs=[HBM] * 4,
        out_specs=[VMEM] * 7 + [SMEM] * 2,
        scratch_shapes=[
            pltpu.VMEM(k.shape, k.dtype),
            pltpu.SMEM(columns.shape, jnp.int32),
            pltpu.SMEM((blocks,), jnp.int32),
            pltpu.SMEM((2, blocks), jnp.int32),
            pltpu.SemaphoreType.DMA((2 * blocks + 4,)),
            pltpu.SemaphoreType.DMA((2,)),
            pltpu.SemaphoreType.DMA,
        ],
        cost_estimate=pl.CostEstimate(flops=100663296, bytes_accessed=4194304, transcendentals=0),
        compiler_params=pltpu.CompilerParams(vmem_limit_bytes=LIMIT),
    )(columns, q, k, v)


class Whole:
    def __init__(self, caps, wide, slim, rest, whole, lists_hbm, lists_ref, sems):
        self.parts = (0, wide, caps[0] - caps[1]), (1, slim, 0)
        self.rest, self.whole, self.sem = rest, whole, sems.at[0]
        self.lists = pltpu.make_async_copy(lists_hbm, lists_ref, sems.at[1])

    def left(self, used, skip):
        count = self.whole.shape[0] - used
        return pltpu.make_async_copy(
            self.rest.at[pl.ds(skip * BLOCK, count), :], self.whole.at[pl.ds(used, count), :], self.sem
        )

    def on_core(self, act):
        for core, first, skip in self.parts:

            @pl.when(lax.axis_index("rep") == core)
            def _():
                act(first, skip)

    def start(self):
        self.lists.start()

        def begin(first, skip):
            self.left(first.shape[0], skip).start()
            self.whole[: first.shape[0], :] = first[...]

        self.on_core(begin)

    def wait(self):
        self.on_core(lambda first, skip: self.left(first.shape[0], skip).wait())


def present(scores, entry):
    return scores + jnp.where(entry >= 0, 0.0, -jnp.inf).astype(jnp.float32)


def score_kernel(
    blocks, caps, lists_hbm, q_ref, near_ref, low, high,
    near_far, other_far, wide, slim, rest, exp_ref, sums_ref, sent_ref,
    whole, lists_ref, sems,
):
    gathered = Whole(caps, wide, slim, rest, whole, lists_hbm, lists_ref, sems)
    gathered.start()
    near = near_ref.shape[1]
    sums_ref[...] = jnp.zeros_like(sums_ref)
    gathered.lists.wait()
    for i in range(blocks):
        query = block_rows(q_ref, i)
        for slot, key in enumerate(far_blocks(i, lists_ref, (near_far, other_far))):
            exp_ref[i, near + slot] = present(score(query, key), lists_ref[i, near + slot])
    gathered.wait()
    for i in range(blocks):
        query = block_rows(q_ref, i)
        scores = [near_ref[i, 0]]
        scores.append(score(query, low[...]) if i == 0 else near_ref[i, 1])
        scores.append(score(query, high[...]) if i == blocks - 1 else near_ref[i, 2])
        scores.extend([exp_ref[i, near], exp_ref[i, near + 1]])
        last = score(query, block_rows(whole, lists_ref[i, LISTED + 2]))
        scores.append(present(last, lists_ref[i, near + 2]))
        peak = scores[0]
        for part in scores[1:]:
            peak = jnp.maximum(peak, part)
        peak = jnp.max(peak, axis=1, keepdims=True)
        exps = [jnp.exp(part - peak) for part in scores]
        for slot, value in enumerate(exps):
            exp_ref[i, slot] = value
        scale = 1.0 / row_total(exps)
        add_columns(sums_ref, lists_ref, i, [value * scale for value in exps])
    sent_ref[...] = sums_ref[...].astype(sent_ref.dtype)


def scaled(exp_ref, lists_ref, i, factor_refs):
    parts = []
    for slot in range(exp_ref.shape[1]):
        value = exp_ref[i, slot]
        for factor in factor_refs:
            value = value * factor[pl.ds(jnp.maximum(lists_ref[i, slot], 0), 1), :]
        parts.append(value)
    return parts


def round_kernel(
    blocks, lists_hbm, exp_ref, sum_a, sum_b, factor_ref, sums_ref, sent_ref, lists_ref, sem
):
    load(lists_hbm, lists_ref, sem)
    factor_ref[...] = 1.0 / (sum_a[...] + sum_b[...].astype(jnp.float32))
    sums_ref[...] = jnp.zeros_like(sums_ref)
    for i in range(blocks):
        parts = scaled(exp_ref, lists_ref, i, [factor_ref])
        scale = 1.0 / row_total(parts)
        add_columns(sums_ref, lists_ref, i, [part * scale for part in parts])
    sent_ref[...] = sums_ref[...].astype(sent_ref.dtype)


def output_kernel(
    blocks, caps, lists_hbm, exp_ref, factor_ref, sum_a, sum_b, own, low, high,
    near_far, other_far, wide, slim, rest, out_ref, last_ref, whole, partial_ref, weight_ref,
    lists_ref, sems,
):
    gathered = Whole(caps, wide, slim, rest, whole, lists_hbm, lists_ref, sems)
    gathered.start()
    last_ref[...] = 1.0 / (sum_a[...] + sum_b[...].astype(jnp.float32))
    gathered.lists.wait()
    for i in range(blocks):
        parts = scaled(exp_ref, lists_ref, i, [factor_ref, last_ref])
        scale = 1.0 / row_total(parts)
        values = near_blocks(i, blocks, own, low, high)
        values += far_blocks(i, lists_ref, (near_far, other_far))
        parts = [(part * scale).astype(jnp.bfloat16) for part in parts]
        total = None
        for part, value in zip(parts, values):
            term = jnp.dot(part, value, preferred_element_type=jnp.float32)
            total = term if total is None else total + term
        partial_ref[i] = total
        weight_ref[i] = parts[-1]
    gathered.wait()
    for i in range(blocks):
        value = block_rows(whole, lists_ref[i, LISTED + 2])
        total = partial_ref[i] + jnp.dot(weight_ref[i], value, preferred_element_type=jnp.float32)
        out_ref[pl.ds(i * BLOCK, BLOCK), :] = total.astype(out_ref.dtype)


def shifted(x, axis, by):
    devices = lax.axis_size(axis)
    return lax.ppermute(x, axis, [(i, (i + by) % devices) for i in range(devices)])


def swapped(x):
    return lax.ppermute(x, "rep", [(0, 1), (1, 0)])


def over_seq(mine, sent):
    devices = lax.axis_size("seq")
    pairs = lambda by: [(i, i ^ by) for i in range(devices)]
    if devices <= 4:
        parts = [lax.ppermute(sent, "seq", pairs(by)) for by in (3, 1, 2) if by < devices]
        return sum([part.astype(mine.dtype) for part in parts], mine)
    by = 1
    while by < devices:
        mine = mine + lax.ppermute(mine, "seq", pairs(by))
        by *= 2
    return mine


def two_away(wide, slim):
    chips = lax.axis_size("seq")
    moves = [(i, (i - 2) % chips) for i in range(chips)]
    axes = ("seq", "rep")
    return (
        lax.ppermute(wide, axes, [(2 * i, 2 * j) for i, j in moves]),
        lax.ppermute(slim, axes, [(2 * i + 1, 2 * j + 1) for i, j in moves]),
    )


def remainder(crowded, *rest):
    return lax.cond(
        crowded,
        lambda *x: tuple(shifted(part, "seq", -2) for part in x),
        lambda *x: x,
        *rest,
    )


def with_swap(near, wide, rest, caps, rep):
    beyond = jnp.concatenate([wide, rest[(caps[0] - caps[1]) * BLOCK :]], axis=0)
    return swapped(jnp.where(rep == 0, beyond, near))


def body(queries, key_rows, value_rows, pattern):
    tok_local, heads_local, width = queries.shape
    assert heads_local == 1
    blocks = tok_local // BLOCK
    list_len = pattern.shape[1]
    far_count = list_len - 3
    total_blocks = pattern.shape[0]
    axes = ("seq", "rep")
    shards = lax.axis_size(axes)
    rep = lax.axis_index("rep")
    q = queries.reshape(tok_local, width)
    k = key_rows.reshape(tok_local, width)
    v = value_rows.reshape(tok_local, width)

    caps = (blocks - blocks // 8, blocks - blocks // 2)
    columns = pattern.T
    k_near = shifted(k, "seq", -1)
    k_wide, k_slim, k_rest = pack_keys(blocks, shards, caps, columns, k)
    k_in, columns, k_wide, k_slim, k_rest = lax.optimization_barrier(
        (k, columns, k_wide, k_slim, k_rest)
    )
    *v_packs, edges_low, edges_high, near_scores, q_held, lists, crowded = plan(
        blocks, shards, caps, columns, q, k_in, v
    )
    v_wide, v_slim, v_rest = v_packs
    k_wide, k_slim = two_away(k_wide, k_slim)
    k_rest, v_rest = remainder(crowded[0] > 0, k_rest, v_rest)
    low = shifted(edges_low, axes, 1)
    high = shifted(edges_high, axes, -1)

    near_scores, v_in = lax.optimization_barrier((near_scores, v))
    v_near = shifted(v_in, "seq", -1)
    k_near, k_wide, k_slim = lax.optimization_barrier((k_near, k_wide, k_slim))
    k_other = with_swap(k_near, k_wide, k_rest, caps, rep)
    exps, sums, sent = pl.pallas_call(
        lambda *refs: score_kernel(blocks, caps, *refs),
        out_shape=(
            jax.ShapeDtypeStruct((blocks, list_len, BLOCK, BLOCK), jnp.float32),
            jax.ShapeDtypeStruct((total_blocks, BLOCK), jnp.float32),
            jax.ShapeDtypeStruct((total_blocks, BLOCK), SENT),
        ),
        in_specs=[HBM] + [VMEM] * 8 + [ANY],
        out_specs=(VMEM, VMEM, VMEM),
        scratch_shapes=[
            pltpu.VMEM((tok_local, width), jnp.bfloat16),
            pltpu.SMEM((blocks, 2 * list_len - 3), jnp.int32),
            pltpu.SemaphoreType.DMA((2,)),
        ],
        cost_estimate=pl.CostEstimate(flops=100663296, bytes_accessed=6291456, transcendentals=786432),
        compiler_params=pltpu.CompilerParams(vmem_limit_bytes=LIMIT),
    )(
        lists, q_held, near_scores, low[:, :width], high[:, :width],
        k_near, k_other, k_wide, k_slim, k_rest,
    )

    v_wide, v_slim, sent = lax.optimization_barrier((v_wide, v_slim, sent))
    mine = over_seq(sums, sent)
    v_wide, v_slim = two_away(v_wide, v_slim)
    mine, v_near = lax.optimization_barrier((mine, v_near))
    v_wide, v_slim = lax.optimization_barrier((v_wide, v_slim))
    factor, sums, sent = pl.pallas_call(
        lambda *refs: round_kernel(blocks, *refs),
        out_shape=(
            jax.ShapeDtypeStruct((total_blocks, BLOCK), jnp.float32),
            jax.ShapeDtypeStruct((total_blocks, BLOCK), jnp.float32),
            jax.ShapeDtypeStruct((total_blocks, BLOCK), SENT),
        ),
        in_specs=[HBM] + [VMEM] * 3,
        out_specs=(VMEM, VMEM, VMEM),
        scratch_shapes=[
            pltpu.SMEM((blocks, 2 * list_len - 3), jnp.int32),
            pltpu.SemaphoreType.DMA,
        ],
        cost_estimate=pl.CostEstimate(flops=7864320, bytes_accessed=4194304, transcendentals=0),
        compiler_params=pltpu.CompilerParams(vmem_limit_bytes=LIMIT),
    )(lists, exps, mine, swapped(mine))

    v_far, factor = lax.optimization_barrier(((v_near, v_wide, v_rest), factor))
    v_near, v_wide, v_rest = v_far
    v_other = with_swap(v_near, v_wide, v_rest, caps, rep)
    mine = over_seq(sums, sent)
    out = pl.pallas_call(
        lambda *refs: output_kernel(blocks, caps, *refs),
        out_shape=jax.ShapeDtypeStruct((tok_local, width), jnp.bfloat16),
        in_specs=[HBM] + [VMEM] * 11 + [ANY],
        out_specs=VMEM,
        scratch_shapes=[
            pltpu.VMEM((total_blocks, BLOCK), jnp.float32),
            pltpu.VMEM((tok_local, width), jnp.bfloat16),
            pltpu.VMEM((blocks, BLOCK, width), jnp.float32),
            pltpu.VMEM((blocks, BLOCK, BLOCK), jnp.bfloat16),
            pltpu.SMEM((blocks, 2 * list_len - 3), jnp.int32),
            pltpu.SemaphoreType.DMA((2,)),
        ],
        cost_estimate=pl.CostEstimate(flops=201326592, bytes_accessed=6291456, transcendentals=0),
        compiler_params=pltpu.CompilerParams(vmem_limit_bytes=LIMIT),
    )(
        lists, exps, factor, mine, swapped(mine), v, low[:, width:], high[:, width:],
        v_near, v_other, v_wide, v_slim, v_rest,
    )
    return out.reshape(tok_local, heads_local, width)


def solution(mesh):
    in_specs = (
        P(("groups", "seq", "rep"), "head", None),
        P(("groups", "seq", "rep"), "head", None),
        P(("groups", "seq", "rep"), "head", None),
        P("groups", None),
    )
    out_specs = P(("groups", "seq", "rep"), "head", None)
    return jax.shard_map(body, mesh=mesh, in_specs=in_specs, out_specs=out_specs, check_vma=False)
```
